256 devices in a mesh: table: 32 (over y, z), tensor: 8 (over x, core).
Axes of the slice: x: 4, y: 4, z: 8, core: 2. Of those that a mesh axis runs over, the one named last changes fastest.
Arguments:
- table_rows: bfloat16 [131072, 256], P('table'), may hold values from -60 to 60
- hist_owner: int32 [64, 512], P('table', 'tensor'), may hold values from 0 to 31, as said below
- hist_row: int32 [64, 512], P('table', 'tensor'), may hold values from 0 to 4095
- ln_gain: float32 [256], replicated, may hold values from 0.1 to 1.9
- w_proj: bfloat16 [256, 16, 256], P(None, 'tensor'), may hold values from -0.375 to 0.375
- norm_gain: float32 [16, 64], P('tensor'), may hold values from 0.1 to 1.9
- w_out: bfloat16 [16, 64, 256], P('tensor'), may hold values from -0.1875 to 0.1875
- w_ckv: bfloat16 [256, 16, 128], P(None, 'tensor'), may hold values from -0.375 to 0.375
- candidates: bfloat16 [16384, 256], P('table'), may hold values from -6 to 6
- cand_group: int32 [128], P('table'), may hold values from 0 to 31, as said below
- cand_member: int32 [128], P('table'), may hold values from 0 to 1
- block_mask: int32 [128, 4], P('table'), may hold values 0 or 1
- w_cq: bfloat16 [256, 16, 64], P(None, 'tensor'), may hold values from -0.375 to 0.375
- w_co: bfloat16 [16, 64, 256], P('tensor'), may hold values from -0.1875 to 0.1875
- w_mlp: bfloat16 [256, 1024], P(None, 'tensor'), may hold values from -0.375 to 0.375
- w_score: bfloat16 [1024], P('tensor'), may hold values from -0.1875 to 0.1875
Outputs:
- states: bfloat16 [64, 512, 256], P('table', 'tensor')
- scores: float32 [16384], P('table')
The draws below stay inside these ranges and needn't reach their ends.
Inputs may be any that keep to these rules, and one draw needn't show every extreme that they name: `hist_owner`: in each device's block of 2 users by 64 positions, at most 8 entries name one slab. `cand_group`: among the 4 candidate blocks of one index of table, at most 1 name one group.
All inputs are finite; a program needn't handle non-finite values. No bound on the sum of `block_mask` on one device may be relied on, other than what follows from the above.
Results may differ from the reference program's by a relative error of at most 0.017.
Values may be sent and summed in bfloat16 or wider, within the bound.
A program may use at most 64 MiB of HBM per device.

```python
import math
import jax
import jax.numpy as jnp
from jax import lax

D = 256
H = 16
DH = 64
MH = 1024
HB = 128
CB = 128
U_DEV = 2
HIST = 512
SLAB = 4096
NSLAB = 32
NSPLIT = 8
USERS = 64
ITEMS = 131072
NCAND = 16384
NBD = 4
BCAP = 1
NBLK = 128
NHB = 4
LBLK = 64
FETCH = 128
CAP = 8


def bounded_owners(key, blocks, rows, owners, capacity):
    hot_owner = jax.random.randint(jax.random.fold_in(key, 1), (), 0, owners).astype(jnp.int32)
    block_keys = jax.random.split(jax.random.fold_in(key, 2), blocks)
    others = (jnp.arange((owners - 1) * capacity, dtype=jnp.int32) // capacity + 1 + hot_owner) % owners

    def one_block(block_key):
        first_key, second_key = jax.random.split(block_key)
        picked = jax.random.permutation(first_key, others)[:rows - capacity]
        filled = jnp.concatenate([jnp.full((capacity,), hot_owner, jnp.int32), picked.astype(jnp.int32)])
        return jax.random.permutation(second_key, filled)
    return jax.vmap(one_block)(block_keys).astype(jnp.int32)


def draw_hist_owner(key, part):
    key = jax.random.fold_in(key, 3)
    flat = bounded_owners(key, NSLAB * NSPLIT, FETCH, NSLAB, CAP)
    shaped = flat.reshape(NSLAB, NSPLIT, U_DEV, LBLK).transpose(0, 2, 1, 3)
    return shaped.reshape(USERS, HIST).astype(jnp.int32)


def draw_cand_group(key, part):
    key = jax.random.fold_in(key, 5)
    return bounded_owners(key, NSLAB, NBD, NSLAB, BCAP).reshape(NBLK).astype(jnp.int32)


def draw_table_rows(key, part):
    key = jax.random.fold_in(key, 7)
    scale_key, base_key = jax.random.split(key, 2)
    row_scale = jnp.exp(jax.random.uniform(scale_key, (ITEMS, 1), jnp.float32) * jnp.log(10.0))
    base = jax.random.truncated_normal(base_key, -5.0, 5.0, (ITEMS, D), jnp.float32)
    return (base * row_scale).astype(jnp.bfloat16)


def touch_ends(result, stream_key, smallest, top_value):
    extent = result.shape
    place = [jax.random.randint(jax.random.fold_in(stream_key, axis), (), 0, extent[axis]) for axis in range(len(extent))]
    result = result.at[tuple(place)].set(smallest)
    longest = extent.index(max(extent))
    place[longest] = (place[longest] + 1) % extent[longest]
    return result.at[tuple(place)].set(top_value)


def shard_levels(rng, extent, shards, low, top_value):
    level, own = 1.0, jax.random.fold_in(rng, 6)
    for axis_at, blocks in shards:
        draws = jnp.exp(jax.random.uniform(jax.random.fold_in(own, axis_at), (blocks,), jnp.float32, low / len(shards), top_value / len(shards)))
        level = level * jnp.repeat(draws, extent[axis_at] // blocks).reshape([-1 if axis == axis_at else 1 for axis in range(len(extent))])
    return level


def scatter_about(key, shape, width, reach, pieces=(), held_as=jnp.bfloat16):
    level = shard_levels(key, shape, pieces, -0.22, 0.18) if pieces else 1.0
    array = jax.random.normal(key, shape, jnp.float32) * width * level
    return jnp.minimum(jnp.maximum(array, -reach), reach).astype(held_as)


def setup_inputs(seed: int = 0) -> dict:
    key_of = jax.random.split(jax.random.key(seed), 17)
    return {
        "table_rows": draw_table_rows(jax.random.fold_in(key_of[16], 71), 0),
        "hist_owner": draw_hist_owner(jax.random.fold_in(key_of[16], 71), 0),
        "hist_row": touch_ends(jax.random.randint(key_of[2], (USERS, HIST), 0, SLAB), jax.random.fold_in(key_of[2], 1), 0, SLAB - 1).astype(jnp.int32),
        "ln_gain": jnp.clip(1.0 + 0.18 * jax.random.normal(key_of[3], (D,), jnp.float32), 0.1, 1.9),
        "w_proj": scatter_about(key_of[4], (D, H, 4 * DH), D ** -0.5, 0.375, ((1, 8),)),
        "norm_gain": jnp.clip(1.0 + 0.18 * jax.random.normal(key_of[5], (H, DH), jnp.float32), 0.1, 1.9),
        "w_out": scatter_about(key_of[6], (H, DH, D), (H * DH) ** -0.5, 0.1875, ((0, 8),)),
        "w_ckv": scatter_about(key_of[7], (D, H, 2 * DH), D ** -0.5, 0.375, ((1, 8),)),
        "candidates": scatter_about(key_of[8], (NCAND, D), 1.0, 6.0, ((0, 32),)),
        "cand_group": draw_cand_group(jax.random.fold_in(key_of[16], 71), 0),
        "cand_member": touch_ends(jax.random.randint(key_of[10], (NBLK,), 0, U_DEV), jax.random.fold_in(key_of[10], 1), 0, U_DEV - 1).astype(jnp.int32),
        "block_mask": touch_ends((jax.random.randint(key_of[11], (NBLK, NHB), 0, 2) < 1).astype(jnp.int32), jax.random.fold_in(key_of[11], 1), 0, 1),
        "w_cq": scatter_about(key_of[12], (D, H, DH), D ** -0.5, 0.375, ((1, 8),)),
        "w_co": scatter_about(key_of[13], (H, DH, D), (H * DH) ** -0.5, 0.1875, ((0, 8),)),
        "w_mlp": scatter_about(key_of[14], (D, MH), D ** -0.5, 0.375, ((1, 8),)),
        "w_score": scatter_about(key_of[15], (MH,), MH ** -0.5, 0.1875, ((0, 8),)),
    }


def normalize(values_f32, gain_vec):
    mean_val = lax.optimization_barrier(jnp.mean(values_f32, axis=-1, keepdims=True))
    centred = values_f32 - mean_val
    var_val = lax.optimization_barrier(jnp.mean(centred * centred, axis=-1, keepdims=True))
    return centred * lax.rsqrt(var_val + 1e-05) * gain_vec

def reference(table_rows, hist_owner, hist_row, ln_gain, w_proj, norm_gain, w_out, w_ckv, candidates, cand_group, cand_member, block_mask, w_cq, w_co, w_mlp, w_score):
    scale_head = 1.0 / math.sqrt(DH)
    scale_hist = 1.0 / math.sqrt(HIST)
    flat_index = (hist_owner * SLAB + hist_row).reshape(USERS * HIST).astype(jnp.int32)
    history = jnp.take(table_rows, flat_index, axis=0).reshape(USERS, HIST, D)
    allowed = jnp.arange(HIST)[None, :] <= jnp.arange(HIST)[:, None]

    def one_user(user_rows):
        rows_f32 = user_rows.astype(jnp.float32)
        normed = normalize(rows_f32, ln_gain).astype(jnp.bfloat16)
        projected = jax.nn.silu(jnp.einsum('td,dhe->the', normed.astype(jnp.float32), w_proj.astype(jnp.float32))).astype(jnp.bfloat16)
        gate_u = projected[..., :DH]
        values = projected[..., DH:2 * DH]
        queries = projected[..., 2 * DH:3 * DH]
        keys = projected[..., 3 * DH:]
        scores = jnp.einsum('qhd,khd->hqk', queries.astype(jnp.float32), keys.astype(jnp.float32)) * scale_head
        weights = jnp.where(allowed[None], jax.nn.silu(scores), 0.0).astype(jnp.bfloat16)
        attended = jnp.einsum('hqk,khd->qhd', weights.astype(jnp.float32), values.astype(jnp.float32))
        gated = (normalize(attended, norm_gain) * gate_u.astype(jnp.float32)).astype(jnp.bfloat16)
        output_sum = jnp.einsum('qhe,hed->qd', gated.astype(jnp.float32), w_out.astype(jnp.float32))
        return (rows_f32 + output_sum).astype(jnp.bfloat16)
    states = lax.map(one_user, history)

    def user_kv(user_states):
        return jnp.einsum('sd,dhe->she', user_states.astype(jnp.float32), w_ckv.astype(jnp.float32)).astype(jnp.bfloat16)
    cross_kv = lax.map(user_kv, states)
    cand_queries = jnp.einsum('cd,dhe->che', candidates.astype(jnp.float32), w_cq.astype(jnp.float32)).astype(jnp.bfloat16)
    query_blocks = cand_queries.reshape(NBLK, CB, H, DH)
    block_users = (cand_group * U_DEV + cand_member).astype(jnp.int32)

    def one_block(items):
        query_block, user_index, mask_row = items
        user_kv_rows = lax.dynamic_index_in_dim(cross_kv, user_index, 0, keepdims=False)
        keys_sel = user_kv_rows[..., :DH].astype(jnp.float32)
        values_sel = user_kv_rows[..., DH:].astype(jnp.float32)
        scores = jnp.einsum('chd,khd->hck', query_block.astype(jnp.float32), keys_sel) * scale_head
        position_mask = jnp.repeat(mask_row, HB).astype(jnp.float32)
        weights = (jax.nn.silu(scores) * position_mask[None, None, :] * scale_hist).astype(jnp.bfloat16)
        return jnp.einsum('hck,khd->chd', weights.astype(jnp.float32), values_sel).astype(jnp.bfloat16)
    cross = lax.map(one_block, (query_blocks, block_users, block_mask)).reshape(NCAND, H, DH)
    cross_sum = jnp.einsum('che,hed->cd', cross.astype(jnp.float32), w_co.astype(jnp.float32))
    mixed = (candidates.astype(jnp.float32) + cross_sum).astype(jnp.bfloat16)
    hidden = jax.nn.silu(jnp.dot(mixed, w_mlp, preferred_element_type=jnp.float32)).astype(jnp.bfloat16)
    scores_out = jnp.dot(hidden, w_score, preferred_element_type=jnp.float32)
    return (states, scores_out)
```

```python
import functools
import math

import jax
import jax.numpy as jnp
from jax import lax
from jax.experimental import pallas as pl
from jax.experimental.pallas import tpu as pltpu
from jax.sharding import PartitionSpec as P

MESH = pl.DeviceIdType.MESH
F32, BF, I32 = jnp.float32, jnp.bfloat16, jnp.int32
A_OUT, A_KV, A_CQ, A_CO, A_MLP, A_SCORE, A_NORM, A_STATE = range(8)
S_MSG, S_REPLY, S_CAND, S_SCORE = range(4)


def dot(a, b):
    return lax.dot_general(a, b, (((1,), (0,)), ((), ())), preferred_element_type=F32)


def dot_nt(a, b):
    return lax.dot_general(a, b, (((1,), (1,)), ((), ())), preferred_element_type=F32)


def iota(shape, axis):
    return lax.broadcasted_iota(I32, shape, axis)


def silu_of_double(half):
    return half + half * jnp.tanh(half)


def kernel(
    T,
    K,
    SLAB,
    CAP,
    group_s,
    member_s,
    mask_s,
    owner_ref,
    row_ref,
    lngain_ref,
    wproj_ref,
    ngain_ref,
    wckv_ref,
    cand_ref,
    wscore_ref,
    table_hbm,
    wout_hbm,
    wcq_hbm,
    wco_hbm,
    wmlp_hbm,
    states_ref,
    scores_ref,
    tab,
    msg,
    m1,
    rep,
    replies,
    csend,
    call,
    wperm,
    wo_all,
    wkv_all,
    wcq_all,
    wco_all,
    wm_all,
    ws_all,
    hist_scr,
    nall,
    pg,
    pv,
    pq,
    pk,
    gs,
    gall,
    sall,
    q2,
    k2,
    v2,
    mb,
    um,
    cr,
    sr,
    rr,
    sc,
    lsem,
    tsend,
    trecv,
    asend,
    arecv,
    gsend,
    grecv,
    fsend,
    frecv,
):
    t, k = lax.axis_index("table"), lax.axis_index("tensor")
    X = K // 2
    x, core = k // 2, k % 2
    sib = k + 1 - 2 * core
    HIST = 64 * K
    R = T * 16
    CB = 16 * K
    NT = R // min(R, 128)
    TR = min(R, 128)
    SHIFT = SLAB.bit_length() - 1

    def local(i, src, dst):
        return pltpu.make_async_copy(src, dst, lsem.at[i])

    locals_ = [
        local(0, table_hbm, tab),
        local(1, wout_hbm, wo_all.at[k]),
        local(2, wcq_hbm, wcq_all.at[k]),
        local(3, wco_hbm, wco_all.at[k]),
        local(4, wmlp_hbm, wm_all.at[k]),
    ]
    for c in locals_:
        c.start()

    barrier = pltpu.get_barrier_semaphore()

    def greet(d, carry):
        pl.semaphore_signal(barrier, inc=1, device_id=(lax.rem(t + d, T), k), device_id_type=MESH)
        return carry

    lax.fori_loop(1, T, greet, 0)
    for d in range(1, K):
        pl.semaphore_signal(barrier, inc=1, device_id=(t, lax.rem(k + d, K)), device_id_type=MESH)

    def over_table(stage, src_of, buf):
        def one(d, carry):
            peer = lax.rem(t + d, T)
            pltpu.make_async_remote_copy(
                src_ref=src_of(peer),
                dst_ref=buf.at[t],
                send_sem=tsend.at[stage, peer],
                recv_sem=trecv.at[stage, t],
                device_id=(peer, k),
                device_id_type=MESH,
            ).start()
            return carry

        lax.fori_loop(1, T, one, 0)

    def table_wait(stage, buf, sends):
        def one(d, carry):
            peer = lax.rem(t + T - d, T)
            copy = pltpu.make_async_remote_copy(
                src_ref=buf.at[peer],
                dst_ref=buf.at[peer],
                send_sem=tsend.at[stage, peer],
                recv_sem=trecv.at[stage, peer],
                device_id=(peer, k),
                device_id_type=MESH,
            )
            if sends:
                copy.wait_send()
            else:
                copy.wait_recv()
            return carry

        lax.fori_loop(1, T, one, 0)

    order = sorted(range(1, X), key=lambda d: min(d, X - d))

    def gather_copy(a, src, buf, chunk, slot, dest):
        return pltpu.make_async_remote_copy(
            src_ref=src,
            dst_ref=buf.at[chunk],
            send_sem=asend.at[a, slot],
            recv_sem=arecv.at[a, chunk],
            device_id=(t, dest),
            device_id_type=MESH,
        )

    def gather_start(a, src, buf):
        for n, d in enumerate(order):
            gather_copy(a, src, buf, k, n, lax.rem(x + d, X) * 2 + core).start()
        gather_copy(a, src, buf, k, X - 1, sib).start()

    def gather_recv(a, buf, chunk):
        gather_copy(a, buf.at[chunk], buf, chunk, 0, sib).wait_recv()

    def near(n):
        return lax.rem(x + X - order[n], X) * 2 + core

    def far(n):
        return lax.rem(x + X - order[n], X) * 2 + 1 - core

    def gather_pass(a, buf, n):
        chunk = near(n)
        gather_recv(a, buf, chunk)
        gather_copy(a, buf.at[chunk], buf, chunk, X + n, sib).start()

    def gather_pass_all(a, buf):
        for n in range(X - 1):
            gather_pass(a, buf, n)

    def gather_rest(a, buf):
        gather_recv(a, buf, sib)
        for n in range(X - 1):
            gather_recv(a, buf, far(n))

    def gather_drain(a, buf):
        for slot in range(2 * X - 1):
            gather_copy(a, buf.at[k], buf, k, slot, sib).wait_send()

    ids = owner_ref[...] * SLAB + row_ref[...]
    own_row = jnp.concatenate([ids[0:1], ids[1:2]], axis=1)
    lane1 = iota((1, 128), 1)
    meta = jnp.zeros((1, 128), I32)
    for b in range(4):
        meta = jnp.where(lane1 == b, group_s[b], meta)
        meta = jnp.where(lane1 == 4 + b, member_s[b], meta)
        for q in range(4):
            meta = jnp.where(lane1 == 8 + 4 * b + q, mask_s[b, q], meta)
    msg[0:1, :] = own_row
    msg[1:2, :] = meta
    m1[t] = msg[...]

    pl.semaphore_wait(barrier, T - 1 + K - 1)
    over_table(S_MSG, lambda peer: msg, m1)

    gather_start(A_OUT, wout_hbm, wo_all)
    wckv = wckv_ref[...]
    kv0, kv1 = wckv[:, 0, :], wckv[:, 1, :]
    wkv_all[k] = jnp.concatenate([kv0[:, :64], kv1[:, :64], kv0[:, 64:], kv1[:, 64:]], axis=1)
    gather_start(A_KV, wkv_all.at[k], wkv_all)
    wproj = wproj_ref[...]
    w0, w1 = wproj[:, 0, :], wproj[:, 1, :]
    half_w = [w[:, 64 * i : 64 * i + 64] for i in range(4) for w in (w0, w1)]
    wperm[...] = jnp.concatenate(half_w, axis=1) * 0.5
    ws_all[k] = jnp.broadcast_to(wscore_ref[...].astype(F32).reshape(1, 128), (8, 128))

    upper = (iota((128, 128), 0) < iota((128, 128), 1)).astype(BF)
    own_slab = own_row >> SHIFT
    hot = iota((T, 128), 0) == own_slab
    rank = dot(hot.astype(BF), upper)
    slot_row = jnp.sum(jnp.where(hot, rank, 0.0), axis=0, keepdims=True) + own_slab.astype(F32) * (2 * CAP)
    eye = iota((128, 128), 0) == iota((128, 128), 1)
    slot_col = jnp.sum(jnp.where(eye, slot_row, 0.0), axis=1, keepdims=True).astype(I32)
    spots = iota((128, 2 * CAP * T), 1)
    pick_left = (spots == slot_col).astype(BF)
    pick_right = (spots == slot_col + CAP).astype(BF)

    table_wait(S_MSG, m1, False)
    wanted_ids = m1[:, 0, :]
    mine = (wanted_ids >> SHIFT) == t
    rank_in = dot(mine.astype(BF), upper)
    low = (wanted_ids & (SLAB - 1)).astype(F32)
    lane_t = iota((T, 128), 1)
    want = jnp.zeros((T, 128), F32)
    for r in range(CAP):
        of_r = jnp.sum(jnp.where(mine & (rank_in == r), low, 0.0), axis=1, keepdims=True)
        want = jnp.where(lane_t == r, of_r, want)
    want_i = want.astype(I32)
    spread = (iota((T * CAP, T), 0) // CAP == iota((T * CAP, T), 1)).astype(BF)
    high = dot(spread, (want_i >> 6).astype(F32).astype(BF))
    lower = dot(spread, (want_i & 63).astype(F32).astype(BF))
    in_lane = iota((T * CAP, 128), 1) == iota((T * CAP, 128), 0) % CAP
    want_col = jnp.sum(jnp.where(in_lane, high * 64.0 + lower, 0.0), axis=1, keepdims=True).astype(I32)
    locals_[0].wait()
    CH = min(512, SLAB)
    rows = jnp.zeros((T * CAP, 256), F32)
    at = iota((T * CAP, CH), 1)
    for c in range(SLAB // CH):
        rows += dot((at == want_col - c * CH).astype(BF), tab[c * CH : (c + 1) * CH, :])
    left = rows[:, :128].reshape(T, CAP, 128)
    right = rows[:, 128:].reshape(T, CAP, 128)
    rep[...] = jnp.concatenate([left, right], axis=1).astype(BF)
    replies[t] = rep[t]
    over_table(S_REPLY, lambda peer: rep.at[peer], replies)

    mine_c = jnp.concatenate(
        [cand_ref[pl.ds(pl.multiple_of(b * CB + 16 * k, 16), 16), :] for b in range(4)], axis=0
    )
    row_c, col_c = iota((R, 64), 0), iota((R, 64), 1)
    col_group = jnp.zeros((R, 64), I32)
    for b in range(4):
        col_group = jnp.where((col_c >> 4) == b, group_s[b], col_group)
    pick_c = ((row_c >> 4) == col_group) & ((row_c & 15) == (col_c & 15))
    csend[...] = dot(pick_c.astype(BF), mine_c).astype(BF).reshape(T, 16, 256)
    call[t] = csend[t]
    over_table(S_CAND, lambda peer: csend.at[peer], call)

    metas = m1[:, 1, :].astype(F32)

    def meta_lane(n):
        return jnp.sum(jnp.where(lane_t == n, metas, 0.0), axis=1, keepdims=True)

    here = [(meta_lane(b) == t.astype(F32)).astype(F32) for b in range(4)]
    member = sum(here[b] * meta_lane(4 + b) for b in range(4))
    reads = [sum(here[b] * meta_lane(8 + 4 * b + q) for b in range(4)) for q in range(4)]
    by_row = (iota((R, T), 0) >> 4 == iota((R, T), 1)).astype(BF)
    um[...] = dot(by_row, jnp.broadcast_to(member, (T, 128)).astype(BF))
    part = iota((T, HIST), 1) // (HIST // 4)
    reads_wide = jnp.zeros((T, HIST), F32)
    for q in range(4):
        reads_wide = jnp.where(part == q, reads[q], reads_wide)
    mb[...] = dot(by_row, reads_wide.astype(BF)).astype(BF)

    table_wait(S_REPLY, replies, False)
    got = replies[...].reshape(T * 2 * CAP, 128)
    history = jnp.concatenate([dot(pick_left, got), dot(pick_right, got)], axis=1)
    hist_scr[...] = history
    centred = history - jnp.mean(history, axis=1, keepdims=True)
    spread_v = jnp.mean(centred * centred, axis=1, keepdims=True)
    nall[k] = (centred * lax.rsqrt(spread_v + 1e-5) * lngain_ref[...]).astype(BF)
    gather_start(A_NORM, nall.at[k], nall)

    def project(chunk):
        half = dot(nall[chunk], wperm[...])
        out = silu_of_double(half).astype(BF)
        place = pl.ds(pl.multiple_of(chunk * 64, 64), 64)
        for n, ref in enumerate((pg, pv, pq, pk)):
            for u in range(2):
                ref[u, place, :] = out[64 * u : 64 * u + 64, 128 * n : 128 * n + 128]

    project(k)
    gather_recv(A_NORM, nall, sib)
    project(sib)
    for n in range(X - 1):
        gather_pass(A_NORM, nall, n)
        project(near(n))
    for n in range(X - 1):
        gather_recv(A_NORM, nall, far(n))
        project(far(n))

    gather_pass_all(A_OUT, wo_all)
    gather_pass_all(A_KV, wkv_all)
    gather_start(A_CQ, wcq_hbm, wcq_all)

    lane = iota((128, 128), 1)
    first = lane < 64
    same_half = jnp.where((iota((128, 128), 0) < 64) == first, 1.0 / 64, 0.0).astype(BF)
    causal = (iota((256, 128), 0) & 127) >= iota((256, 128), 1)
    gain_row = jnp.concatenate([ngain_ref[0:1, :], ngain_ref[1:2, :]], axis=1)
    zero = jnp.zeros((128, 128), BF)

    def gated_copy(u, piece, source):
        return pltpu.make_async_remote_copy(
            src_ref=gs.at[u, piece],
            dst_ref=gall.at[u, source],
            send_sem=gsend.at[u, piece],
            recv_sem=grecv.at[u, source],
            device_id=(t, piece),
            device_id_type=MESH,
        )

    for u in range(2):
        for block in range(HIST // 128):
            start = block * 128
            queries = pq[u, start : start + 128, :] * 0.0625
            both = jnp.concatenate([jnp.where(first, queries, zero), jnp.where(first, zero, queries)], axis=0)
            half = dot_nt(both, pk[u, start : start + 128, :])
            weights = jnp.where(causal, silu_of_double(half), 0.0).astype(BF)
            total = dot(weights, pv[u, start : start + 128, :])
            if block:
                weights = silu_of_double(dot_nt(both, pk[u, :start, :])).astype(BF)
                total += dot(weights, pv[u, :start, :])
            attended = jnp.where(first, total[:128], total[128:])
            coarse = attended.astype(BF)
            fine = (attended - coarse.astype(F32)).astype(BF)
            off = attended - (dot(coarse, same_half) + dot(fine, same_half))
            spread_a = dot((off * off).astype(BF), same_half)
            gate = pg[u, start : start + 128, :].astype(F32)
            gated = (off * lax.rsqrt(spread_a + 1e-5) * gain_row * gate).astype(BF)
            gs[u, 2 * block] = gated[:64]
            gs[u, 2 * block + 1] = gated[64:]
        gall[u, k] = gs[u, k]
        for d in range(1, K):
            gated_copy(u, lax.rem(k + d, K), k).start()

    gather_pass_all(A_CQ, wcq_all)
    table_wait(S_CAND, call, False)
    gather_rest(A_CQ, wcq_all)
    locals_[2].wait()
    first_r = iota((TR, 128), 1) < 64
    zero_r = jnp.zeros((TR, 128), BF)

    def make_queries(j, carry):
        for tile in range(NT):
            cands = call[tile * (TR // 16) : (tile + 1) * (TR // 16)].reshape(TR, 256)
            queries = dot_nt(cands, wcq_all[j]).astype(BF) * 0.0625
            one = um[tile * TR : (tile + 1) * TR, :] > 0.5
            parts = (jnp.where(one, zero_r, queries), jnp.where(one, queries, zero_r))
            q2[j, tile, :TR, :] = jnp.concatenate([jnp.where(first_r, q, zero_r) for q in parts], axis=1)
            q2[j, tile, TR:, :] = jnp.concatenate([jnp.where(first_r, zero_r, q) for q in parts], axis=1)
        return carry

    lax.fori_loop(0, K, make_queries, 0)

    gather_rest(A_OUT, wo_all)
    locals_[1].wait()
    for u in range(2):
        for d in range(1, K):
            source = lax.rem(k + K - d, K)
            gated_copy(u, source, source).wait_recv()
    total = hist_scr[...]
    for m in range(X):
        pair = [jnp.concatenate([gall[u, 2 * m], gall[u, 2 * m + 1]], axis=1) for u in range(2)]
        total += dot(jnp.concatenate(pair, axis=0), wo_all[2 * m : 2 * m + 2].reshape(256, 256))
    states = total.astype(BF)
    sall[k] = states
    gather_start(A_STATE, sall.at[k], sall)
    states_ref[...] = states.reshape(2, 64, 256)
    gather_start(A_CO, wco_hbm, wco_all)
    gather_start(A_MLP, wmlp_hbm, wm_all)
    gather_start(A_SCORE, ws_all.at[k], ws_all)

    gather_rest(A_KV, wkv_all)

    def make_kv(chunk):
        place = pl.ds(pl.multiple_of(chunk * 64, 64), 64)
        rows_s = sall[chunk]
        for j in range(K):
            kv = dot(rows_s, wkv_all[j]).astype(BF)
            for u in range(2):
                k2[j, place, 128 * u : 128 * u + 128] = kv[64 * u : 64 * u + 64, :128]
                v2[j, place, 128 * u : 128 * u + 128] = kv[64 * u : 64 * u + 64, 128:]

    make_kv(k)
    gather_recv(A_STATE, sall, sib)
    make_kv(sib)
    for n in range(X - 1):
        gather_pass(A_STATE, sall, n)
        make_kv(near(n))
    for n in range(X - 1):
        gather_recv(A_STATE, sall, far(n))
        make_kv(far(n))

    gather_pass_all(A_CO, wco_all)
    gather_pass_all(A_MLP, wm_all)
    gather_pass_all(A_SCORE, ws_all)

    def cross_pair(j, carry):
        for tile in range(NT):
            reads_t = mb[tile * TR : (tile + 1) * TR, :]
            half = dot_nt(q2[j, tile], k2[j])
            weights = silu_of_double(half).astype(BF)
            weights = jnp.concatenate([weights[:TR] * reads_t, weights[TR:] * reads_t], axis=0)
            out = dot(weights, v2[j])
            one = um[tile * TR : (tile + 1) * TR, :] > 0.5
            top = jnp.where(one, out[:TR, 128:], out[:TR, :128])
            bottom = jnp.where(one, out[TR:, 128:], out[TR:, :128])
            got_c = jnp.where(first_r, top, bottom) * (1.0 / math.sqrt(HIST))
            cr[j, tile * TR : (tile + 1) * TR, :] = got_c.astype(BF)
        return carry

    lax.fori_loop(0, K, cross_pair, 0)

    gather_rest(A_CO, wco_all)
    gather_rest(A_MLP, wm_all)
    gather_rest(A_SCORE, ws_all)
    locals_[3].wait()
    locals_[4].wait()
    mixed = call[...].reshape(R, 256).astype(F32)
    for m in range(X):
        pair = jnp.concatenate([cr[2 * m], cr[2 * m + 1]], axis=1)
        mixed += dot(pair, wco_all[2 * m : 2 * m + 2].reshape(256, 256))
    mixed = mixed.astype(BF)
    total_s = jnp.zeros((R, 128), F32)
    for m in range(X):
        half = dot(mixed, jnp.concatenate([wm_all[2 * m], wm_all[2 * m + 1]], axis=1)) * 0.5
        hidden = silu_of_double(half).astype(BF).astype(F32)
        total_s += hidden[:, :128] * ws_all[2 * m][0:1, :] + hidden[:, 128:] * ws_all[2 * m + 1][0:1, :]
    score = jnp.sum(total_s, axis=1, keepdims=True)
    at_lane = (iota((R, 128), 0) & 15) == (iota((R, 128), 1) & 15)
    by_slot = jnp.sum(jnp.where(at_lane, score, 0.0).reshape(T, 16, 128), axis=1)
    sr[...] = by_slot.reshape(T, 1, 128)
    rr[t] = sr[t]
    over_table(S_SCORE, lambda peer: sr.at[peer], rr)
    table_wait(S_SCORE, rr, False)
    back = rr[...].reshape(T, 128)
    groups = iota((T, 128), 0)
    own_lanes = (lane1 >> 4) == k
    blocks = [jnp.sum(jnp.where(groups == group_s[b], back, 0.0), axis=0, keepdims=True) for b in range(4)]
    sc[k] = jnp.where(own_lanes, jnp.concatenate(blocks, axis=0), 0.0)

    def score_copy(dest, source, slot):
        return pltpu.make_async_remote_copy(
            src_ref=sc.at[source],
            dst_ref=sc.at[source],
            send_sem=fsend.at[slot],
            recv_sem=frecv.at[source],
            device_id=(t, dest),
            device_id_type=MESH,
        )

    for d in range(1, K):
        score_copy(lax.rem(k + d, K), k, d).start()

    table_wait(S_MSG, m1, True)
    table_wait(S_REPLY, replies, True)
    table_wait(S_CAND, call, True)
    table_wait(S_SCORE, rr, True)
    for a, buf in (
        (A_OUT, wo_all),
        (A_KV, wkv_all),
        (A_CQ, wcq_all),
        (A_CO, wco_all),
        (A_MLP, wm_all),
        (A_SCORE, ws_all),
        (A_NORM, nall),
        (A_STATE, sall),
    ):
        gather_drain(a, buf)
    for u in range(2):
        for d in range(1, K):
            gated_copy(u, lax.rem(k + d, K), k).wait_send()
    for d in range(1, K):
        score_copy(lax.rem(k + d, K), k, d).wait_send()
    for d in range(1, K):
        source = lax.rem(k + K - d, K)
        score_copy(source, source, d).wait_recv()
    final = sc[0]
    for n in range(1, K):
        final += sc[n]
    scores_ref[...] = final


def body(
    T,
    K,
    table_rows,
    hist_owner,
    hist_row,
    ln_gain,
    w_proj,
    norm_gain,
    w_out,
    w_ckv,
    candidates,
    cand_group,
    cand_member,
    block_mask,
    w_cq,
    w_co,
    w_mlp,
    w_score,
):
    slab = table_rows.shape[0]
    cap = max(1, 2 * hist_owner.size // T)
    rows, hist = 16 * T, 64 * K
    tile = min(rows, 128)
    vmem, smem, anyspace = (
        pl.BlockSpec(memory_space=pltpu.VMEM),
        pl.BlockSpec(memory_space=pltpu.SMEM),
        pl.BlockSpec(memory_space=pl.ANY),
    )
    scratch = [
        pltpu.VMEM((slab, 256), BF),
        pltpu.VMEM((2, 128), I32),
        pltpu.VMEM((T, 2, 128), I32),
        pltpu.VMEM((T, 2 * cap, 128), BF),
        pltpu.VMEM((T, 2 * cap, 128), BF),
        pltpu.VMEM((T, 16, 256), BF),
        pltpu.VMEM((T, 16, 256), BF),
        pltpu.VMEM((256, 512), BF),
        pltpu.VMEM((K, 128, 256), BF),
        pltpu.VMEM((K, 256, 256), BF),
        pltpu.VMEM((K, 128, 256), BF),
        pltpu.VMEM((K, 128, 256), BF),
        pltpu.VMEM((K, 256, 128), BF),
        pltpu.VMEM((K, 8, 128), F32),
        pltpu.VMEM((128, 256), F32),
        pltpu.VMEM((K, 128, 256), BF),
        pltpu.VMEM((2, hist, 128), BF),
        pltpu.VMEM((2, hist, 128), BF),
        pltpu.VMEM((2, hist, 128), BF),
        pltpu.VMEM((2, hist, 128), BF),
        pltpu.VMEM((2, K, 64, 128), BF),
        pltpu.VMEM((2, K, 64, 128), BF),
        pltpu.VMEM((K, 128, 256), BF),
        pltpu.VMEM((K, rows // tile, 2 * tile, 256), BF),
        pltpu.VMEM((K, hist, 256), BF),
        pltpu.VMEM((K, hist, 256), BF),
        pltpu.VMEM((rows, hist), BF),
        pltpu.VMEM((rows, 128), F32),
        pltpu.VMEM((K, rows, 128), BF),
        pltpu.VMEM((T, 1, 128), F32),
        pltpu.VMEM((T, 1, 128), F32),
        pltpu.VMEM((K, 4, 128), F32),
        pltpu.SemaphoreType.DMA((5,)),
        pltpu.SemaphoreType.DMA((4, T)),
        pltpu.SemaphoreType.DMA((4, T)),
        pltpu.SemaphoreType.DMA((8, K)),
        pltpu.SemaphoreType.DMA((8, K)),
        pltpu.SemaphoreType.DMA((2, K)),
        pltpu.SemaphoreType.DMA((2, K)),
        pltpu.SemaphoreType.DMA((K,)),
        pltpu.SemaphoreType.DMA((K,)),
    ]
    states, scores = pl.pallas_call(
        functools.partial(kernel, T, K, slab, cap),
        out_shape=(
            jax.ShapeDtypeStruct((2, 64, 256), BF),
            jax.ShapeDtypeStruct((4, 128), F32),
        ),
        in_specs=[smem] * 3 + [vmem] * 8 + [anyspace] * 5,
        out_specs=(vmem, vmem),
        scratch_shapes=scratch,
        compiler_params=pltpu.CompilerParams(
            collective_id=0, has_side_effects=True, vmem_limit_bytes=48 * 1024 * 1024
        ),
    )(
        cand_group,
        cand_member,
        block_mask,
        hist_owner,
        hist_row,
        ln_gain.reshape(1, 256),
        w_proj,
        norm_gain,
        w_ckv,
        candidates,
        w_score.reshape(1, 128),
        table_rows,
        w_out.reshape(128, 256),
        jnp.transpose(w_cq, (1, 2, 0)).reshape(128, 256),
        w_co.reshape(128, 256),
        w_mlp,
    )
    return states, scores[:, : 16 * K].reshape(4 * 16 * K)


def solution(mesh):
    T, K = mesh.shape["table"], mesh.shape["tensor"]
    return jax.shard_map(
        functools.partial(body, T, K),
        mesh=mesh,
        in_specs=(
            P("table", None),
            P("table", "tensor"),
            P("table", "tensor"),
            P(),
            P(None, "tensor", None),
            P("tensor", None),
            P("tensor", None, None),
            P(None, "tensor", None),
            P("table", None),
            P("table"),
            P("table"),
            P("table", None),
            P(None, "tensor", None),
            P("tensor", None, None),
            P(None, "tensor"),
            P("tensor"),
        ),
        out_specs=(P("table", "tensor", None), P("table")),
        check_vma=False,
    )
```

```python
import functools
import math

import jax
import jax.numpy as jnp
from jax import lax
from jax.experimental import pallas as pl
from jax.experimental.pallas import tpu as pltpu
from jax.sharding import PartitionSpec as P

MESH = pl.DeviceIdType.MESH
F32, BF, I32 = jnp.float32, jnp.bfloat16, jnp.int32
A_OUT, A_KV, A_CQ, A_CO, A_MLP, A_SCORE, A_NORM, A_STATE = range(8)
S_MSG, S_REPLY, S_CAND, S_SCORE = range(4)


def dot(a, b):
    return lax.dot_general(a, b, (((1,), (0,)), ((), ())), preferred_element_type=F32)


def dot_nt(a, b):
    return lax.dot_general(a, b, (((1,), (1,)), ((), ())), preferred_element_type=F32)


def iota(shape, axis):
    return lax.broadcasted_iota(I32, shape, axis)


def silu_of_double(half):
    return half + half * jnp.tanh(half)


def kernel(
    T,
    K,
    SLAB,
    CAP,
    group_hbm,
    member_hbm,
    mask_hbm,
    owner_hbm,
    row_hbm,
    lngain_hbm,
    wproj_hbm,
    ngain_hbm,
    wckv_hbm,
    cand_hbm,
    wscore_hbm,
    table_hbm,
    wout_hbm,
    wcq_hbm,
    wco_hbm,
    wmlp_hbm,
    states_ref,
    scores_ref,
    group_s,
    member_s,
    mask_s,
    owner_ref,
    row_ref,
    lngain_ref,
    wproj_ref,
    ngain_ref,
    wckv_ref,
    cand_ref,
    wscore_ref,
    tab,
    msg,
    m1,
    rep,
    replies,
    csend,
    call,
    wperm,
    wo_all,
    wkv_all,
    wcq_all,
    wco_all,
    wm_all,
    ws_all,
    hist_scr,
    nall,
    pg,
    pv,
    pq,
    pk,
    gs,
    gall,
    sall,
    q2,
    k2,
    v2,
    mb,
    um,
    cr,
    sr,
    rr,
    sc,
    lsem,
    tsend,
    trecv,
    asend,
    arecv,
    gsend,
    grecv,
    fsend,
    frecv,
):
    t, k = lax.axis_index("table"), lax.axis_index("tensor")
    X = K // 2
    x, core = k // 2, k % 2
    sib = k + 1 - 2 * core
    HIST = 64 * K
    R = T * 16
    CB = 16 * K
    NT = R // min(R, 128)
    TR = min(R, 128)
    SHIFT = SLAB.bit_length() - 1

    def local(i, src, dst):
        return pltpu.make_async_copy(src, dst, lsem.at[i])

    locals_ = [
        local(0, table_hbm, tab),
        local(1, wout_hbm, wo_all.at[k]),
        local(2, wcq_hbm, wcq_all.at[k]),
        local(3, wco_hbm, wco_all.at[k]),
        local(4, wmlp_hbm, wm_all.at[k]),
    ]
    ids_in = [
        local(5, owner_hbm, owner_ref),
        local(6, row_hbm, row_ref),
        local(7, group_hbm, group_s),
        local(8, member_hbm, member_s),
        local(9, mask_hbm, mask_s),
    ]
    weights_in = [
        local(10, wckv_hbm, wckv_ref),
        local(11, wproj_hbm, wproj_ref),
        local(12, wscore_hbm, wscore_ref),
    ]
    late_in = [
        local(13, cand_hbm, cand_ref),
        local(14, lngain_hbm, lngain_ref),
        local(15, ngain_hbm, ngain_ref),
    ]
    for c in ids_in + weights_in + locals_ + late_in:
        c.start()

    barrier = pltpu.get_barrier_semaphore()

    def greet(d, carry):
        pl.semaphore_signal(barrier, inc=1, device_id=(lax.rem(t + d, T), k), device_id_type=MESH)
        return carry

    lax.fori_loop(1, T, greet, 0)
    for d in range(1, K):
        pl.semaphore_signal(barrier, inc=1, device_id=(t, lax.rem(k + d, K)), device_id_type=MESH)

    def over_table(stage, src_of, buf):
        def one(d, carry):
            peer = lax.rem(t + d, T)
            pltpu.make_async_remote_copy(
                src_ref=src_of(peer),
                dst_ref=buf.at[t],
                send_sem=tsend.at[stage, peer],
                recv_sem=trecv.at[stage, t],
                device_id=(peer, k),
                device_id_type=MESH,
            ).start()
            return carry

        lax.fori_loop(1, T, one, 0)

    def table_wait(stage, buf, sends):
        def one(d, carry):
            peer = lax.rem(t + T - d, T)
            copy = pltpu.make_async_remote_copy(
                src_ref=buf.at[peer],
                dst_ref=buf.at[peer],
                send_sem=tsend.at[stage, peer],
                recv_sem=trecv.at[stage, peer],
                device_id=(peer, k),
                device_id_type=MESH,
            )
            if sends:
                copy.wait_send()
            else:
                copy.wait_recv()
            return carry

        lax.fori_loop(1, T, one, 0)

    order = sorted(range(1, X), key=lambda d: min(d, X - d))

    def gather_copy(a, src, buf, chunk, slot, dest):
        return pltpu.make_async_remote_copy(
            src_ref=src,
            dst_ref=buf.at[chunk],
            send_sem=asend.at[a, slot],
            recv_sem=arecv.at[a, chunk],
            device_id=(t, dest),
            device_id_type=MESH,
        )

    def gather_start(a, src, buf):
        for n, d in enumerate(order):
            gather_copy(a, src, buf, k, n, lax.rem(x + d, X) * 2 + core).start()
        gather_copy(a, src, buf, k, X - 1, sib).start()

    def gather_recv(a, buf, chunk):
        gather_copy(a, buf.at[chunk], buf, chunk, 0, sib).wait_recv()

    def near(n):
        return lax.rem(x + X - order[n], X) * 2 + core

    def far(n):
        return lax.rem(x + X - order[n], X) * 2 + 1 - core

    def gather_pass(a, buf, n):
        chunk = near(n)
        gather_recv(a, buf, chunk)
        gather_copy(a, buf.at[chunk], buf, chunk, X + n, sib).start()

    def gather_pass_all(a, buf):
        for n in range(X - 1):
            gather_pass(a, buf, n)

    def gather_rest(a, buf):
        gather_recv(a, buf, sib)
        for n in range(X - 1):
            gather_recv(a, buf, far(n))

    def gather_drain(a, buf):
        for slot in range(2 * X - 1):
            gather_copy(a, buf.at[k], buf, k, slot, sib).wait_send()

    for c in ids_in:
        c.wait()
    ids = owner_ref[...] * SLAB + row_ref[...]
    own_row = jnp.concatenate([ids[0:1], ids[1:2]], axis=1)
    lane1 = iota((1, 128), 1)
    meta = jnp.zeros((1, 128), I32)
    for b in range(4):
        meta = jnp.where(lane1 == b, group_s[b], meta)
        meta = jnp.where(lane1 == 4 + b, member_s[b], meta)
        for q in range(4):
            meta = jnp.where(lane1 == 8 + 4 * b + q, mask_s[b, q], meta)
    msg[0:1, :] = own_row
    msg[1:2, :] = meta
    m1[t] = msg[...]

    pl.semaphore_wait(barrier, T - 1 + K - 1)
    over_table(S_MSG, lambda peer: msg, m1)

    gather_start(A_OUT, wout_hbm, wo_all)
    for c in weights_in:
        c.wait()
    wckv = wckv_ref[...]
    kv0, kv1 = wckv[:, 0, :], wckv[:, 1, :]
    wkv_all[k] = jnp.concatenate([kv0[:, :64], kv1[:, :64], kv0[:, 64:], kv1[:, 64:]], axis=1)
    gather_start(A_KV, wkv_all.at[k], wkv_all)
    wproj = wproj_ref[...]
    w0, w1 = wproj[:, 0, :], wproj[:, 1, :]
    half_w = [w[:, 64 * i : 64 * i + 64] for i in range(4) for w in (w0, w1)]
    wperm[...] = jnp.concatenate(half_w, axis=1) * 0.5
    ws_all[k] = jnp.broadcast_to(wscore_ref[...].astype(F32).reshape(1, 128), (8, 128))

    upper = (iota((128, 128), 0) < iota((128, 128), 1)).astype(BF)
    own_slab = own_row >> SHIFT
    hot = iota((T, 128), 0) == own_slab
    rank = dot(hot.astype(BF), upper)
    slot_row = jnp.sum(jnp.where(hot, rank, 0.0), axis=0, keepdims=True) + own_slab.astype(F32) * (2 * CAP)
    eye = iota((128, 128), 0) == iota((128, 128), 1)
    slot_col = jnp.sum(jnp.where(eye, slot_row, 0.0), axis=1, keepdims=True).astype(I32)
    spots = iota((128, 2 * CAP * T), 1)
    pick_left = (spots == slot_col).astype(BF)
    pick_right = (spots == slot_col + CAP).astype(BF)

    table_wait(S_MSG, m1, False)
    wanted_ids = m1[:, 0, :]
    mine = (wanted_ids >> SHIFT) == t
    rank_in = dot(mine.astype(BF), upper)
    low = (wanted_ids & (SLAB - 1)).astype(F32)
    lane_t = iota((T, 128), 1)
    want = jnp.zeros((T, 128), F32)
    for r in range(CAP):
        of_r = jnp.sum(jnp.where(mine & (rank_in == r), low, 0.0), axis=1, keepdims=True)
        want = jnp.where(lane_t == r, of_r, want)
    want_i = want.astype(I32)
    spread = (iota((T * CAP, T), 0) // CAP == iota((T * CAP, T), 1)).astype(BF)
    high = dot(spread, (want_i >> 6).astype(F32).astype(BF))
    lower = dot(spread, (want_i & 63).astype(F32).astype(BF))
    in_lane = iota((T * CAP, 128), 1) == iota((T * CAP, 128), 0) % CAP
    want_col = jnp.sum(jnp.where(in_lane, high * 64.0 + lower, 0.0), axis=1, keepdims=True).astype(I32)
    locals_[0].wait()
    CH = min(512, SLAB)
    rows = jnp.zeros((T * CAP, 256), F32)
    at = iota((T * CAP, CH), 1)
    for c in range(SLAB // CH):
        rows += dot((at == want_col - c * CH).astype(BF), tab[c * CH : (c + 1) * CH, :])
    left = rows[:, :128].reshape(T, CAP, 128)
    right = rows[:, 128:].reshape(T, CAP, 128)
    rep[...] = jnp.concatenate([left, right], axis=1).astype(BF)
    replies[t] = rep[t]
    over_table(S_REPLY, lambda peer: rep.at[peer], replies)

    for c in late_in:
        c.wait()
    mine_c = jnp.concatenate(
        [cand_ref[pl.ds(pl.multiple_of(b * CB + 16 * k, 16), 16), :] for b in range(4)], axis=0
    )
    row_c, col_c = iota((R, 64), 0), iota((R, 64), 1)
    col_group = jnp.zeros((R, 64), I32)
    for b in range(4):
        col_group = jnp.where((col_c >> 4) == b, group_s[b], col_group)
    pick_c = ((row_c >> 4) == col_group) & ((row_c & 15) == (col_c & 15))
    csend[...] = dot(pick_c.astype(BF), mine_c).astype(BF).reshape(T, 16, 256)
    call[t] = csend[t]
    over_table(S_CAND, lambda peer: csend.at[peer], call)

    metas = m1[:, 1, :].astype(F32)

    def meta_lane(n):
        return jnp.sum(jnp.where(lane_t == n, metas, 0.0), axis=1, keepdims=True)

    here = [(meta_lane(b) == t.astype(F32)).astype(F32) for b in range(4)]
    member = sum(here[b] * meta_lane(4 + b) for b in range(4))
    reads = [sum(here[b] * meta_lane(8 + 4 * b + q) for b in range(4)) for q in range(4)]
    by_row = (iota((R, T), 0) >> 4 == iota((R, T), 1)).astype(BF)
    um[...] = dot(by_row, jnp.broadcast_to(member, (T, 128)).astype(BF))
    part = iota((T, HIST), 1) // (HIST // 4)
    reads_wide = jnp.zeros((T, HIST), F32)
    for q in range(4):
        reads_wide = jnp.where(part == q, reads[q], reads_wide)
    mb[...] = dot(by_row, reads_wide.astype(BF)).astype(BF)

    table_wait(S_REPLY, replies, False)
    got = replies[...].reshape(T * 2 * CAP, 128)
    history = jnp.concatenate([dot(pick_left, got), dot(pick_right, got)], axis=1)
    hist_scr[...] = history
    centred = history - jnp.mean(history, axis=1, keepdims=True)
    spread_v = jnp.mean(centred * centred, axis=1, keepdims=True)
    nall[k] = (centred * lax.rsqrt(spread_v + 1e-5) * lngain_ref[...]).astype(BF)
    gather_start(A_NORM, nall.at[k], nall)

    def project(chunk):
        half = dot(nall[chunk], wperm[...])
        out = silu_of_double(half).astype(BF)
        place = pl.ds(pl.multiple_of(chunk * 64, 64), 64)
        for n, ref in enumerate((pg, pv, pq, pk)):
            for u in range(2):
                ref[u, place, :] = out[64 * u : 64 * u + 64, 128 * n : 128 * n + 128]

    project(k)
    gather_recv(A_NORM, nall, sib)
    project(sib)
    for n in range(X - 1):
        gather_pass(A_NORM, nall, n)
        project(near(n))
    for n in range(X - 1):
        gather_recv(A_NORM, nall, far(n))
        project(far(n))

    gather_pass_all(A_OUT, wo_all)
    gather_pass_all(A_KV, wkv_all)
    gather_start(A_CQ, wcq_hbm, wcq_all)

    lane = iota((128, 128), 1)
    first = lane < 64
    same_half = jnp.where((iota((128, 128), 0) < 64) == first, 1.0 / 64, 0.0).astype(BF)
    causal = (iota((256, 128), 0) & 127) >= iota((256, 128), 1)
    gain_row = jnp.concatenate([ngain_ref[0:1, :], ngain_ref[1:2, :]], axis=1)
    zero = jnp.zeros((128, 128), BF)

    def gated_copy(u, piece, source):
        return pltpu.make_async_remote_copy(
            src_ref=gs.at[u, piece],
            dst_ref=gall.at[u, source],
            send_sem=gsend.at[u, piece],
            recv_sem=grecv.at[u, source],
            device_id=(t, piece),
            device_id_type=MESH,
        )

    for u in range(2):
        for block in range(HIST // 128):
            start = block * 128
            queries = pq[u, start : start + 128, :] * 0.0625
            both = jnp.concatenate([jnp.where(first, queries, zero), jnp.where(first, zero, queries)], axis=0)
            half = dot_nt(both, pk[u, start : start + 128, :])
            weights = jnp.where(causal, silu_of_double(half), 0.0).astype(BF)
            total = dot(weights, pv[u, start : start + 128, :])
            if block:
                weights = silu_of_double(dot_nt(both, pk[u, :start, :])).astype(BF)
                total += dot(weights, pv[u, :start, :])
            attended = jnp.where(first, total[:128], total[128:])
            coarse = attended.astype(BF)
            fine = (attended - coarse.astype(F32)).astype(BF)
            off = attended - (dot(coarse, same_half) + dot(fine, same_half))
            spread_a = dot((off * off).astype(BF), same_half)
            gate = pg[u, start : start + 128, :].astype(F32)
            gated = (off * lax.rsqrt(spread_a + 1e-5) * gain_row * gate).astype(BF)
            gs[u, 2 * block] = gated[:64]
            gs[u, 2 * block + 1] = gated[64:]
        gall[u, k] = gs[u, k]
        for d in range(1, K):
            gated_copy(u, lax.rem(k + d, K), k).start()

    gather_pass_all(A_CQ, wcq_all)
    table_wait(S_CAND, call, False)
    gather_rest(A_CQ, wcq_all)
    locals_[2].wait()
    first_r = iota((TR, 128), 1) < 64
    zero_r = jnp.zeros((TR, 128), BF)

    def make_queries(j, carry):
        for tile in range(NT):
            cands = call[tile * (TR // 16) : (tile + 1) * (TR // 16)].reshape(TR, 256)
            queries = dot_nt(cands, wcq_all[j]).astype(BF) * 0.0625
            one = um[tile * TR : (tile + 1) * TR, :] > 0.5
            parts = (jnp.where(one, zero_r, queries), jnp.where(one, queries, zero_r))
            q2[j, tile, :TR, :] = jnp.concatenate([jnp.where(first_r, q, zero_r) for q in parts], axis=1)
            q2[j, tile, TR:, :] = jnp.concatenate([jnp.where(first_r, zero_r, q) for q in parts], axis=1)
        return carry

    lax.fori_loop(0, K, make_queries, 0)

    gather_rest(A_OUT, wo_all)
    locals_[1].wait()
    for u in range(2):
        for d in range(1, K):
            source = lax.rem(k + K - d, K)
            gated_copy(u, source, source).wait_recv()
    total = hist_scr[...]
    for m in range(X):
        pair = [jnp.concatenate([gall[u, 2 * m], gall[u, 2 * m + 1]], axis=1) for u in range(2)]
        total += dot(jnp.concatenate(pair, axis=0), wo_all[2 * m : 2 * m + 2].reshape(256, 256))
    states = total.astype(BF)
    sall[k] = states
    gather_start(A_STATE, sall.at[k], sall)
    states_ref[...] = states.reshape(2, 64, 256)
    gather_start(A_CO, wco_hbm, wco_all)
    gather_start(A_MLP, wmlp_hbm, wm_all)
    gather_start(A_SCORE, ws_all.at[k], ws_all)

    gather_rest(A_KV, wkv_all)

    def make_kv(chunk):
        place = pl.ds(pl.multiple_of(chunk * 64, 64), 64)
        rows_s = sall[chunk]
        for j in range(K):
            kv = dot(rows_s, wkv_all[j]).astype(BF)
            for u in range(2):
                k2[j, place, 128 * u : 128 * u + 128] = kv[64 * u : 64 * u + 64, :128]
                v2[j, place, 128 * u : 128 * u + 128] = kv[64 * u : 64 * u + 64, 128:]

    make_kv(k)
    gather_recv(A_STATE, sall, sib)
    make_kv(sib)
    for n in range(X - 1):
        gather_pass(A_STATE, sall, n)
        make_kv(near(n))
    for n in range(X - 1):
        gather_recv(A_STATE, sall, far(n))
        make_kv(far(n))

    gather_pass_all(A_CO, wco_all)
    gather_pass_all(A_MLP, wm_all)
    gather_pass_all(A_SCORE, ws_all)

    def cross_pair(j, carry):
        for tile in range(NT):
            reads_t = mb[tile * TR : (tile + 1) * TR, :]
            half = dot_nt(q2[j, tile], k2[j])
            weights = silu_of_double(half).astype(BF)
            weights = jnp.concatenate([weights[:TR] * reads_t, weights[TR:] * reads_t], axis=0)
            out = dot(weights, v2[j])
            one = um[tile * TR : (tile + 1) * TR, :] > 0.5
            top = jnp.where(one, out[:TR, 128:], out[:TR, :128])
            bottom = jnp.where(one, out[TR:, 128:], out[TR:, :128])
            got_c = jnp.where(first_r, top, bottom) * (1.0 / math.sqrt(HIST))
            cr[j, tile * TR : (tile + 1) * TR, :] = got_c.astype(BF)
        return carry

    lax.fori_loop(0, K, cross_pair, 0)

    gather_rest(A_CO, wco_all)
    gather_rest(A_MLP, wm_all)
    gather_rest(A_SCORE, ws_all)
    locals_[3].wait()
    locals_[4].wait()
    mixed = call[...].reshape(R, 256).astype(F32)
    for m in range(X):
        pair = jnp.concatenate([cr[2 * m], cr[2 * m + 1]], axis=1)
        mixed += dot(pair, wco_all[2 * m : 2 * m + 2].reshape(256, 256))
    mixed = mixed.astype(BF)
    total_s = jnp.zeros((R, 128), F32)
    for m in range(X):
        half = dot(mixed, jnp.concatenate([wm_all[2 * m], wm_all[2 * m + 1]], axis=1)) * 0.5
        hidden = silu_of_double(half).astype(BF).astype(F32)
        total_s += hidden[:, :128] * ws_all[2 * m][0:1, :] + hidden[:, 128:] * ws_all[2 * m + 1][0:1, :]
    score = jnp.sum(total_s, axis=1, keepdims=True)
    at_lane = (iota((R, 128), 0) & 15) == (iota((R, 128), 1) & 15)
    by_slot = jnp.sum(jnp.where(at_lane, score, 0.0).reshape(T, 16, 128), axis=1)
    sr[...] = by_slot.reshape(T, 1, 128)
    rr[t] = sr[t]
    over_table(S_SCORE, lambda peer: sr.at[peer], rr)
    table_wait(S_SCORE, rr, False)
    back = rr[...].reshape(T, 128)
    groups = iota((T, 128), 0)
    own_lanes = (lane1 >> 4) == k
    blocks = [jnp.sum(jnp.where(groups == group_s[b], back, 0.0), axis=0, keepdims=True) for b in range(4)]
    sc[k] = jnp.where(own_lanes, jnp.concatenate(blocks, axis=0), 0.0)

    def score_copy(dest, source, slot):
        return pltpu.make_async_remote_copy(
            src_ref=sc.at[source],
            dst_ref=sc.at[source],
            send_sem=fsend.at[slot],
            recv_sem=frecv.at[source],
            device_id=(t, dest),
            device_id_type=MESH,
        )

    for d in range(1, K):
        score_copy(lax.rem(k + d, K), k, d).start()

    table_wait(S_MSG, m1, True)
    table_wait(S_REPLY, replies, True)
    table_wait(S_CAND, call, True)
    table_wait(S_SCORE, rr, True)
    for a, buf in (
        (A_OUT, wo_all),
        (A_KV, wkv_all),
        (A_CQ, wcq_all),
        (A_CO, wco_all),
        (A_MLP, wm_all),
        (A_SCORE, ws_all),
        (A_NORM, nall),
        (A_STATE, sall),
    ):
        gather_drain(a, buf)
    for u in range(2):
        for d in range(1, K):
            gated_copy(u, lax.rem(k + d, K), k).wait_send()
    for d in range(1, K):
        score_copy(lax.rem(k + d, K), k, d).wait_send()
    for d in range(1, K):
        source = lax.rem(k + K - d, K)
        score_copy(source, source, d).wait_recv()
    final = sc[0]
    for n in range(1, K):
        final += sc[n]
    scores_ref[...] = final


def body(
    T,
    K,
    table_rows,
    hist_owner,
    hist_row,
    ln_gain,
    w_proj,
    norm_gain,
    w_out,
    w_ckv,
    candidates,
    cand_group,
    cand_member,
    block_mask,
    w_cq,
    w_co,
    w_mlp,
    w_score,
):
    slab = table_rows.shape[0]
    cap = max(1, 2 * hist_owner.size // T)
    rows, hist = 16 * T, 64 * K
    tile = min(rows, 128)
    vmem, hbm = pl.BlockSpec(memory_space=pltpu.VMEM), pl.BlockSpec(memory_space=pltpu.HBM)
    scratch = [
        pltpu.SMEM((4,), I32),
        pltpu.SMEM((4,), I32),
        pltpu.SMEM((4, 4), I32),
        pltpu.VMEM((2, 64), I32),
        pltpu.VMEM((2, 64), I32),
        pltpu.VMEM((1, 256), F32),
        pltpu.VMEM((256, 2, 256), BF),
        pltpu.VMEM((2, 64), F32),
        pltpu.VMEM((256, 2, 128), BF),
        pltpu.VMEM((64 * K, 256), BF),
        pltpu.VMEM((1, 128), BF),
        pltpu.VMEM((slab, 256), BF),
        pltpu.VMEM((2, 128), I32),
        pltpu.VMEM((T, 2, 128), I32),
        pltpu.VMEM((T, 2 * cap, 128), BF),
        pltpu.VMEM((T, 2 * cap, 128), BF),
        pltpu.VMEM((T, 16, 256), BF),
        pltpu.VMEM((T, 16, 256), BF),
        pltpu.VMEM((256, 512), BF),
        pltpu.VMEM((K, 128, 256), BF),
        pltpu.VMEM((K, 256, 256), BF),
        pltpu.VMEM((K, 128, 256), BF),
        pltpu.VMEM((K, 128, 256), BF),
        pltpu.VMEM((K, 256, 128), BF),
        pltpu.VMEM((K, 8, 128), F32),
        pltpu.VMEM((128, 256), F32),
        pltpu.VMEM((K, 128, 256), BF),
        pltpu.VMEM((2, hist, 128), BF),
        pltpu.VMEM((2, hist, 128), BF),
        pltpu.VMEM((2, hist, 128), BF),
        pltpu.VMEM((2, hist, 128), BF),
        pltpu.VMEM((2, K, 64, 128), BF),
        pltpu.VMEM((2, K, 64, 128), BF),
        pltpu.VMEM((K, 128, 256), BF),
        pltpu.VMEM((K, rows // tile, 2 * tile, 256), BF),
        pltpu.VMEM((K, hist, 256), BF),
        pltpu.VMEM((K, hist, 256), BF),
        pltpu.VMEM((rows, hist), BF),
        pltpu.VMEM((rows, 128), F32),
        pltpu.VMEM((K, rows, 128), BF),
        pltpu.VMEM((T, 1, 128), F32),
        pltpu.VMEM((T, 1, 128), F32),
        pltpu.VMEM((K, 4, 128), F32),
        pltpu.SemaphoreType.DMA((16,)),
        pltpu.SemaphoreType.DMA((4, T)),
        pltpu.SemaphoreType.DMA((4, T)),
        pltpu.SemaphoreType.DMA((8, K)),
        pltpu.SemaphoreType.DMA((8, K)),
        pltpu.SemaphoreType.DMA((2, K)),
        pltpu.SemaphoreType.DMA((2, K)),
        pltpu.SemaphoreType.DMA((K,)),
        pltpu.SemaphoreType.DMA((K,)),
    ]
    states, scores = pl.pallas_call(
        functools.partial(kernel, T, K, slab, cap),
        out_shape=(
            jax.ShapeDtypeStruct((2, 64, 256), BF),
            jax.ShapeDtypeStruct((4, 128), F32),
        ),
        in_specs=[hbm] * 16,
        out_specs=(vmem, vmem),
        scratch_shapes=scratch,
        compiler_params=pltpu.CompilerParams(
            collective_id=0, has_side_effects=True, vmem_limit_bytes=60 * 1024 * 1024
        ),
    )(
        cand_group,
        cand_member,
        block_mask,
        hist_owner,
        hist_row,
        ln_gain.reshape(1, 256),
        w_proj,
        norm_gain,
        w_ckv,
        candidates,
        w_score.reshape(1, 128),
        table_rows,
        w_out.reshape(128, 256),
        jnp.transpose(w_cq, (1, 2, 0)).reshape(128, 256),
        w_co.reshape(128, 256),
        w_mlp,
    )
    return states, scores[:, : 16 * K].reshape(4 * 16 * K)


def solution(mesh):
    T, K = mesh.shape["table"], mesh.shape["tensor"]
    return jax.shard_map(
        functools.partial(body, T, K),
        mesh=mesh,
        in_specs=(
            P("table", None),
            P("table", "tensor"),
            P("table", "tensor"),
            P(),
            P(None, "tensor", None),
            P("tensor", None),
            P("tensor", None, None),
            P(None, "tensor", None),
            P("table", None),
            P("table"),
            P("table"),
            P("table", None),
            P(None, "tensor", None),
            P("tensor", None, None),
            P(None, "tensor"),
            P("tensor"),
        ),
        out_specs=(P("table", "tensor", None), P("table")),
        check_vma=False,
    )
```

```python
import functools
import math

import jax
import jax.numpy as jnp
from jax import lax
from jax.experimental import pallas as pl
from jax.experimental.pallas import tpu as pltpu
from jax.sharding import PartitionSpec as P

MESH = pl.DeviceIdType.MESH
F32, BF, I32 = jnp.float32, jnp.bfloat16, jnp.int32
A_OUT, A_K, A_V, A_CQ, A_CO, A_MLP, A_SCORE, A_STATE = range(8)
S_MSG, S_REPLY, S_CAND, S_SCORE = range(4)


def dot(a, b):
    return lax.dot_general(a, b, (((1,), (0,)), ((), ())), preferred_element_type=F32)


def dot_nt(a, b):
    return lax.dot_general(a, b, (((1,), (1,)), ((), ())), preferred_element_type=F32)


def iota(shape, axis):
    return lax.broadcasted_iota(I32, shape, axis)


def silu_of_double(half):
    return half + half * jnp.tanh(half)


def kernel(
    T,
    K,
    SLAB,
    CAP,
    group_hbm,
    member_hbm,
    mask_hbm,
    owner_hbm,
    row_hbm,
    lngain_hbm,
    wproj_hbm,
    ngain_hbm,
    wckv_hbm,
    cand_hbm,
    wscore_hbm,
    table_hbm,
    wout_hbm,
    wcq_hbm,
    wco_hbm,
    wmlp_hbm,
    states_ref,
    scores_ref,
    group_s,
    member_s,
    mask_s,
    owner_ref,
    row_ref,
    lngain_ref,
    wproj_ref,
    ngain_ref,
    wckv_ref,
    cand_ref,
    wscore_ref,
    tab,
    msg,
    m1,
    rep,
    replies,
    csend,
    call,
    wperm,
    gains,
    wo_all,
    wk_all,
    wv_all,
    wcq_all,
    wco_all,
    wm_all,
    ws_all,
    hist_scr,
    nown,
    nall,
    pg,
    pv,
    pq,
    pk,
    gs,
    gall,
    sall,
    q2,
    k2,
    v2,
    mb,
    um,
    sr,
    rr,
    sc,
    lsem,
    tsend,
    trecv,
    asend,
    arecv,
    hrecv,
    psend,
    precv,
    nsend,
    nrecv,
    gsend,
    grecv,
    fsend,
    frecv,
):
    t, k = lax.axis_index("table"), lax.axis_index("tensor")
    X = K // 2
    x, core = k // 2, k % 2
    sib = k + 1 - 2 * core
    HIST = 64 * K
    R = T * 16
    CB = 16 * K
    TR = min(R, 256)
    NT = R // TR
    SHIFT = SLAB.bit_length() - 1

    def local(i, src, dst):
        return pltpu.make_async_copy(src, dst, lsem.at[i])

    locals_ = [
        local(0, table_hbm, tab),
        local(1, wout_hbm, wo_all.at[k]),
        local(2, wcq_hbm, wcq_all.at[k]),
        local(3, wco_hbm, wco_all.at[k]),
        local(4, wmlp_hbm, wm_all.at[k]),
    ]
    ids_in = [
        local(5, owner_hbm, owner_ref),
        local(6, row_hbm, row_ref),
        local(7, group_hbm, group_s),
        local(8, member_hbm, member_s),
        local(9, mask_hbm, mask_s),
    ]
    weights_in = [
        local(10, wckv_hbm, wckv_ref),
        local(11, wproj_hbm, wproj_ref),
        local(12, wscore_hbm, wscore_ref),
        local(15, ngain_hbm, ngain_ref),
    ]
    late_in = [
        local(13, cand_hbm, cand_ref),
        local(14, lngain_hbm, lngain_ref),
    ]
    for c in ids_in + weights_in + locals_ + late_in:
        c.start()

    barrier = pltpu.get_barrier_semaphore()

    def greet(d, carry):
        pl.semaphore_signal(barrier, inc=1, device_id=(lax.rem(t + d, T), k), device_id_type=MESH)
        return carry

    lax.fori_loop(1, T, greet, 0)
    for d in range(1, K):
        pl.semaphore_signal(barrier, inc=1, device_id=(t, lax.rem(k + d, K)), device_id_type=MESH)

    def over_table(stage, src_of, buf):
        def one(d, carry):
            peer = lax.rem(t + d, T)
            pltpu.make_async_remote_copy(
                src_ref=src_of(peer),
                dst_ref=buf.at[t],
                send_sem=tsend.at[stage, peer],
                recv_sem=trecv.at[stage, t],
                device_id=(peer, k),
                device_id_type=MESH,
            ).start()
            return carry

        lax.fori_loop(1, T, one, 0)

    def table_wait(stage, buf, sends):
        def one(d, carry):
            peer = lax.rem(t + T - d, T)
            copy = pltpu.make_async_remote_copy(
                src_ref=buf.at[peer],
                dst_ref=buf.at[peer],
                send_sem=tsend.at[stage, peer],
                recv_sem=trecv.at[stage, peer],
                device_id=(peer, k),
                device_id_type=MESH,
            )
            if sends:
                copy.wait_send()
            else:
                copy.wait_recv()
            return carry

        lax.fori_loop(1, T, one, 0)

    order = sorted(range(1, X), key=lambda d: min(d, X - d))

    def gather_copy(a, src, buf, chunk, slot, dest):
        return pltpu.make_async_remote_copy(
            src_ref=src,
            dst_ref=buf.at[chunk],
            send_sem=asend.at[a, slot],
            recv_sem=arecv.at[a, chunk],
            device_id=(t, dest),
            device_id_type=MESH,
        )

    def gather_start(a, src, buf):
        for n, d in enumerate(order):
            gather_copy(a, src, buf, k, n, lax.rem(x + d, X) * 2 + core).start()
        gather_copy(a, src, buf, k, X - 1, sib).start()

    def gather_recv(a, buf, chunk):
        gather_copy(a, buf.at[chunk], buf, chunk, 0, sib).wait_recv()

    def near(n):
        return lax.rem(x + X - order[n], X) * 2 + core

    def far(n):
        return lax.rem(x + X - order[n], X) * 2 + 1 - core

    def gather_pass(a, buf, n):
        chunk = near(n)
        gather_recv(a, buf, chunk)
        gather_copy(a, buf.at[chunk], buf, chunk, X + n, sib).start()

    def gather_rest(a, buf):
        gather_recv(a, buf, sib)
        for n in range(X - 1):
            gather_recv(a, buf, far(n))

    def gather_drain(a, buf):
        for slot in range(2 * X - 1):
            gather_copy(a, buf.at[k], buf, k, slot, sib).wait_send()

    assert X == 4
    right, left = lax.rem(x + 1, X) * 2 + core, lax.rem(x + X - 1, X) * 2 + core
    across = lax.rem(x + 2, X) * 2 + core

    def half_copy(a, buf, chunk, side, dest):
        size = buf.shape[1] // 2
        part = buf.at[chunk, pl.ds(side * size, size)]
        return pltpu.make_async_remote_copy(
            src_ref=part,
            dst_ref=part,
            send_sem=asend.at[a, 3 + side],
            recv_sem=hrecv.at[a, side],
            device_id=(t, dest),
            device_id_type=MESH,
        )

    def relay_start(a, src, buf):
        gather_copy(a, src, buf, k, 0, right).start()
        gather_copy(a, src, buf, k, 1, left).start()
        gather_copy(a, src, buf, k, 2, sib).start()

    def relay_pass(a, buf):
        gather_recv(a, buf, left)
        half_copy(a, buf, left, 0, right).start()
        gather_copy(a, buf.at[left], buf, left, 5, sib).start()
        gather_recv(a, buf, right)
        half_copy(a, buf, right, 1, left).start()
        gather_copy(a, buf.at[right], buf, right, 6, sib).start()

    def relay_finish(a, buf):
        half_copy(a, buf, across, 0, sib).wait_recv()
        half_copy(a, buf, across, 1, sib).wait_recv()
        gather_copy(a, buf.at[across], buf, across, 7, sib).start()

    def relay_drain(a, buf):
        for slot in (0, 1, 2, 5, 6, 7):
            gather_copy(a, buf.at[k], buf, k, slot, sib).wait_send()
        half_copy(a, buf, left, 0, right).wait_send()
        half_copy(a, buf, right, 1, left).wait_send()

    def pair_copy(n, buf, slot):
        return pltpu.make_async_remote_copy(
            src_ref=buf.at[slot],
            dst_ref=buf.at[slot],
            send_sem=psend.at[n],
            recv_sem=precv.at[n],
            device_id=(t, sib),
            device_id_type=MESH,
        )

    for c in ids_in:
        c.wait()
    ids = owner_ref[...] * SLAB + row_ref[...]
    own_row = jnp.concatenate([ids[0:1], ids[1:2]], axis=1)
    lane1 = iota((1, 128), 1)
    meta = jnp.zeros((1, 128), I32)
    for b in range(4):
        meta = jnp.where(lane1 == b, group_s[b], meta)
        meta = jnp.where(lane1 == 4 + b, member_s[b], meta)
        for q in range(4):
            meta = jnp.where(lane1 == 8 + 4 * b + q, mask_s[b, q], meta)
    msg[0:1, :] = own_row
    msg[1:2, :] = meta
    m1[t] = msg[...]

    pl.semaphore_wait(barrier, T - 1 + K - 1)
    over_table(S_MSG, lambda peer: msg, m1)

    relay_start(A_OUT, wout_hbm, wo_all)
    for c in weights_in:
        c.wait()
    wckv = wckv_ref[...]
    kv0, kv1 = wckv[:, 0, :], wckv[:, 1, :]
    wk_all[k] = jnp.concatenate([kv0[:, :64], kv1[:, :64]], axis=1).T
    wv_all[k] = jnp.concatenate([kv0[:, 64:], kv1[:, 64:]], axis=1)
    relay_start(A_K, wk_all.at[k], wk_all)
    relay_start(A_V, wv_all.at[k], wv_all)
    wproj = wproj_ref[...]
    w0, w1 = wproj[:, 0, :], wproj[:, 1, :]
    half_w = [w[:, 64 * i : 64 * i + 64] for i in range(4) for w in (w0, w1)]
    wperm[core] = jnp.concatenate(half_w, axis=1) * 0.5
    gains[core] = jnp.concatenate([ngain_ref[0:1, :], ngain_ref[1:2, :]], axis=1)
    pair_copy(0, wperm, core).start()
    pair_copy(1, gains, core).start()
    ws_all[k] = jnp.broadcast_to(wscore_ref[...].astype(F32).reshape(1, 128), (8, 128))

    upper = (iota((128, 128), 0) < iota((128, 128), 1)).astype(BF)
    own_slab = own_row >> SHIFT
    hot = iota((T, 128), 0) == own_slab
    rank = dot(hot.astype(BF), upper)
    slot_row = jnp.sum(jnp.where(hot, rank, 0.0), axis=0, keepdims=True) + own_slab.astype(F32) * (2 * CAP)
    eye = iota((128, 128), 0) == iota((128, 128), 1)
    slot_col = jnp.sum(jnp.where(eye, slot_row, 0.0), axis=1, keepdims=True).astype(I32)
    spots = iota((128, 2 * CAP * T), 1)
    pick_left = (spots == slot_col).astype(BF)
    pick_right = (spots == slot_col + CAP).astype(BF)

    table_wait(S_MSG, m1, False)
    relay_start(A_CQ, wcq_hbm, wcq_all)
    relay_start(A_CO, wco_hbm, wco_all)
    relay_start(A_MLP, wmlp_hbm, wm_all)
    gather_start(A_SCORE, ws_all.at[k], ws_all)
    wanted_ids = m1[:, 0, :]
    mine = (wanted_ids >> SHIFT) == t
    rank_in = dot(mine.astype(BF), upper)
    low = (wanted_ids & (SLAB - 1)).astype(F32)
    lane_t = iota((T, 128), 1)
    want = jnp.zeros((T, 128), F32)
    for r in range(CAP):
        of_r = jnp.sum(jnp.where(mine & (rank_in == r), low, 0.0), axis=1, keepdims=True)
        want = jnp.where(lane_t == r, of_r, want)
    want_i = want.astype(I32)
    spread = (iota((T * CAP, T), 0) // CAP == iota((T * CAP, T), 1)).astype(BF)
    high = dot(spread, (want_i >> 6).astype(F32).astype(BF))
    lower = dot(spread, (want_i & 63).astype(F32).astype(BF))
    in_lane = iota((T * CAP, 128), 1) == iota((T * CAP, 128), 0) % CAP
    want_col = jnp.sum(jnp.where(in_lane, high * 64.0 + lower, 0.0), axis=1, keepdims=True).astype(I32)
    locals_[0].wait()
    CH = min(512, SLAB)
    rows = jnp.zeros((T * CAP, 256), F32)
    at = iota((T * CAP, CH), 1)
    for c in range(SLAB // CH):
        rows += dot((at == want_col - c * CH).astype(BF), tab[c * CH : (c + 1) * CH, :])
    halves = [rows[:, :128].reshape(T, CAP, 128), rows[:, 128:].reshape(T, CAP, 128)]
    rep[...] = jnp.concatenate(halves, axis=1).astype(BF)
    replies[t] = rep[t]
    over_table(S_REPLY, lambda peer: rep.at[peer], replies)

    relay_pass(A_OUT, wo_all)
    relay_pass(A_K, wk_all)
    relay_pass(A_V, wv_all)

    for c in late_in:
        c.wait()
    mine_c = jnp.concatenate(
        [cand_ref[pl.ds(pl.multiple_of(b * CB + 16 * k, 16), 16), :] for b in range(4)], axis=0
    )
    row_c, col_c = iota((R, 64), 0), iota((R, 64), 1)
    col_group = jnp.zeros((R, 64), I32)
    for b in range(4):
        col_group = jnp.where((col_c >> 4) == b, group_s[b], col_group)
    pick_c = ((row_c >> 4) == col_group) & ((row_c & 15) == (col_c & 15))
    csend[...] = dot(pick_c.astype(BF), mine_c).astype(BF).reshape(T, 16, 256)
    call[t] = csend[t]

    metas = m1[:, 1, :].astype(F32)

    def meta_lane(n):
        return jnp.sum(jnp.where(lane_t == n, metas, 0.0), axis=1, keepdims=True)

    here = [(meta_lane(b) == t.astype(F32)).astype(F32) for b in range(4)]
    member = sum(here[b] * meta_lane(4 + b) for b in range(4))
    reads = [sum(here[b] * meta_lane(8 + 4 * b + q) for b in range(4)) for q in range(4)]
    by_row = (iota((R, T), 0) >> 4 == iota((R, T), 1)).astype(BF)
    um[...] = dot(by_row, jnp.broadcast_to(member, (T, 128)).astype(BF))
    part = (iota((T, HIST), 1) % (HIST // 2)) // (HIST // 8)
    reads_wide = jnp.zeros((T, HIST), F32)
    for q in range(4):
        reads_wide = jnp.where(part == q, reads[q], reads_wide)
    mb[...] = dot(by_row, reads_wide.astype(BF)).astype(BF)

    table_wait(S_REPLY, replies, False)
    got = replies[...].reshape(T * 2 * CAP, 128)
    history = jnp.concatenate([dot(pick_left, got), dot(pick_right, got)], axis=1)
    hist_scr[...] = history
    centred = history - jnp.mean(history, axis=1, keepdims=True)
    spread_v = jnp.mean(centred * centred, axis=1, keepdims=True)
    normed = (centred * lax.rsqrt(spread_v + 1e-5) * lngain_ref[...]).astype(BF)
    nown[0] = normed[:64]
    nown[1] = normed[64:]

    def normed_copy(dest, source):
        return pltpu.make_async_remote_copy(
            src_ref=nown.at[dest % 2],
            dst_ref=nall.at[source],
            send_sem=nsend.at[dest],
            recv_sem=nrecv.at[source],
            device_id=(t, dest),
            device_id_type=MESH,
        )

    def others(n):
        return lax.rem(k + n, K)

    for n in range(1, K):
        normed_copy(others(n), k).start()
    nall[k] = nown[core]
    over_table(S_CAND, lambda peer: csend.at[peer], call)
    pair_copy(0, wperm, 1 - core).wait_recv()
    pair_copy(1, gains, 1 - core).wait_recv()

    def project(chip):
        rows_n = nall[pl.ds(2 * chip, 2)].reshape(128, 256)
        place = pl.ds(pl.multiple_of(chip * 128, 128), 128)
        for p in range(2):
            out = silu_of_double(dot(rows_n, wperm[p])).astype(BF)
            for n, ref in enumerate((pg, pv, pq, pk)):
                ref[p, place, :] = out[:, 128 * n : 128 * n + 128]

    normed_copy(sib, sib).wait_recv()
    project(x)
    for d in order:
        chip = lax.rem(x + d, X)
        for c in range(2):
            normed_copy(2 * chip + c, 2 * chip + c).wait_recv()
        project(chip)
    relay_finish(A_OUT, wo_all)
    relay_finish(A_K, wk_all)
    relay_finish(A_V, wv_all)
    relay_pass(A_CQ, wcq_all)
    relay_pass(A_CO, wco_all)
    relay_pass(A_MLP, wm_all)
    for n in range(X - 1):
        gather_pass(A_SCORE, ws_all, n)

    lane = iota((128, 128), 1)
    first = lane < 64
    same_half = jnp.where((iota((128, 128), 0) < 64) == first, 1.0 / 64, 0.0).astype(BF)
    causal = (iota((256, 128), 0) & 127) >= iota((256, 128), 1)
    zero = jnp.zeros((128, 128), BF)

    def gated_copy(dest, source):
        return pltpu.make_async_remote_copy(
            src_ref=gs.at[dest],
            dst_ref=gall.at[source % 2, source // 2],
            send_sem=gsend.at[dest],
            recv_sem=grecv.at[source],
            device_id=(t, dest),
            device_id_type=MESH,
        )

    for block in range(HIST // 128):
        start = block * 128
        for p in range(2):
            queries = pq[p, start : start + 128, :] * 0.0625
            both = jnp.concatenate([jnp.where(first, queries, zero), jnp.where(first, zero, queries)], axis=0)
            half = dot_nt(both, pk[p, start : start + 128, :])
            weights = jnp.where(causal, silu_of_double(half), 0.0).astype(BF)
            total = dot(weights, pv[p, start : start + 128, :])
            if block:
                weights = silu_of_double(dot_nt(both, pk[p, :start, :])).astype(BF)
                total += dot(weights, pv[p, :start, :])
            attended = jnp.where(first, total[:128], total[128:])
            coarse = attended.astype(BF)
            fine = (attended - coarse.astype(F32)).astype(BF)
            off = attended - (dot(coarse, same_half) + dot(fine, same_half))
            spread_a = dot((off * off).astype(BF), same_half)
            gate = pg[p, start : start + 128, :].astype(F32)
            gated = (off * lax.rsqrt(spread_a + 1e-5) * gains[p] * gate).astype(BF)
            gs[2 * block, :, 128 * p : 128 * p + 128] = gated[:64]
            gs[2 * block + 1, :, 128 * p : 128 * p + 128] = gated[64:]
        for dest in (2 * block, 2 * block + 1):

            @pl.when(k != dest)
            def _():
                gated_copy(dest, k).start()

    gall[core, x] = gs[k]

    relay_finish(A_CQ, wcq_all)
    table_wait(S_CAND, call, False)
    gather_rest(A_CQ, wcq_all)
    locals_[2].wait()
    first_r = iota((TR, 128), 1) < 64
    zero_r = jnp.zeros((TR, 128), BF)

    def make_queries(j, carry):
        for tile in range(NT):
            cands = call[tile * (TR // 16) : (tile + 1) * (TR // 16)].reshape(TR, 256)
            queries = dot_nt(cands, wcq_all[j]).astype(BF) * 0.0625
            one = um[tile * TR : (tile + 1) * TR, :] > 0.5
            parts = (jnp.where(one, zero_r, queries), jnp.where(one, queries, zero_r))
            q2[j, tile, :TR, :] = jnp.concatenate([jnp.where(first_r, q, zero_r) for q in parts], axis=1)
            q2[j, tile, TR:, :] = jnp.concatenate([jnp.where(first_r, zero_r, q) for q in parts], axis=1)
        return carry

    lax.fori_loop(0, K // 2, make_queries, 0)

    gather_rest(A_OUT, wo_all)
    locals_[1].wait()
    for n in range(1, K):
        gated_copy(others(n), others(n)).wait_recv()
    total = hist_scr[...]
    for m in range(X):
        pieces = jnp.concatenate([gall[0, m], gall[1, m]], axis=0)
        total += dot(pieces, wo_all[2 * m : 2 * m + 2].reshape(256, 256))
    states = total.astype(BF)
    sall[k] = states
    gather_start(A_STATE, sall.at[k], sall)
    states_ref[...] = states.reshape(2, 64, 256)
    relay_finish(A_CO, wco_all)
    relay_finish(A_MLP, wm_all)

    lax.fori_loop(K // 2, K, make_queries, 0)

    gather_rest(A_K, wk_all)
    gather_rest(A_V, wv_all)

    def make_kv(part, own):
        place = slice(part * (HIST // 2), (part + 1) * (HIST // 2))
        values_w = jnp.concatenate([wv_all[j] for j in range(K)], axis=1)
        for u in range(2):
            rows_s = jnp.concatenate([sall[2 * m + own, 64 * u : 64 * u + 64, :] for m in range(X)], axis=0)
            keys = dot_nt(wk_all[...].reshape(K * 128, 256), rows_s).astype(BF)
            values = dot(rows_s, values_w).astype(BF)
            for j in range(K):
                k2[j, 128 * u : 128 * u + 128, place] = keys[128 * j : 128 * j + 128]
                v2[j, place, 128 * u : 128 * u + 128] = values[:, 128 * j : 128 * j + 128]

    for n in range(X - 1):
        gather_pass(A_STATE, sall, n)
    make_kv(0, core)
    gather_rest(A_STATE, sall)
    make_kv(1, 1 - core)

    def cross_pair(j, tile):
        tile_rows = pl.ds(pl.multiple_of(tile * TR, TR), TR)
        reads_t = mb[tile_rows, :]
        weights = silu_of_double(dot(q2[j, tile], k2[j])).astype(BF)
        weights = jnp.concatenate([weights[:TR] * reads_t, weights[TR:] * reads_t], axis=0)
        out = dot(weights, v2[j])
        one = um[tile_rows, :] > 0.5
        top = jnp.where(one, out[:TR, 128:], out[:TR, :128])
        bottom = jnp.where(one, out[TR:, 128:], out[TR:, :128])
        return jnp.where(first_r, top, bottom)

    gather_rest(A_CO, wco_all)
    gather_rest(A_MLP, wm_all)
    gather_rest(A_SCORE, ws_all)
    locals_[3].wait()
    locals_[4].wait()
    at_lane = (iota((TR, 128), 0) & 15) == (iota((TR, 128), 1) & 15)
    SLOTS = TR // 16

    def finish_tile(tile, carry):
        mixed = call[pl.ds(tile * SLOTS, SLOTS)].reshape(TR, 256).astype(F32)
        for m in range(X):
            pair = [
                (cross_pair(j, tile) * (1.0 / math.sqrt(HIST))).astype(BF)
                for j in (2 * m, 2 * m + 1)
            ]
            mixed += dot(jnp.concatenate(pair, axis=1), wco_all[2 * m : 2 * m + 2].reshape(256, 256))
        mixed = mixed.astype(BF)
        total_s = jnp.zeros((TR, 128), F32)
        for m in range(X):
            half = dot(mixed, jnp.concatenate([wm_all[2 * m], wm_all[2 * m + 1]], axis=1)) * 0.5
            hidden = silu_of_double(half).astype(BF).astype(F32)
            total_s += hidden[:, :128] * ws_all[2 * m][0:1, :] + hidden[:, 128:] * ws_all[2 * m + 1][0:1, :]
        score = jnp.sum(total_s, axis=1, keepdims=True)
        by_slot = jnp.sum(jnp.where(at_lane, score, 0.0).reshape(SLOTS, 16, 128), axis=1)
        sr[pl.ds(tile * SLOTS, SLOTS)] = by_slot.reshape(SLOTS, 1, 128)
        for i in range(SLOTS):
            slot = tile * SLOTS + i

            @pl.when(slot != t)
            def _():
                pltpu.make_async_remote_copy(
                    src_ref=sr.at[slot],
                    dst_ref=rr.at[t],
                    send_sem=tsend.at[S_SCORE, slot],
                    recv_sem=trecv.at[S_SCORE, t],
                    device_id=(slot, k),
                    device_id_type=MESH,
                ).start()

        return carry

    lax.fori_loop(0, NT, finish_tile, 0)
    rr[t] = sr[t]
    table_wait(S_SCORE, rr, False)
    back = rr[...].reshape(T, 128)
    groups = iota((T, 128), 0)
    own_lanes = (lane1 >> 4) == k
    blocks = [jnp.sum(jnp.where(groups == group_s[b], back, 0.0), axis=0, keepdims=True) for b in range(4)]
    sc[k] = jnp.where(own_lanes, jnp.concatenate(blocks, axis=0), 0.0)

    def score_copy(dest, source, slot):
        return pltpu.make_async_remote_copy(
            src_ref=sc.at[source],
            dst_ref=sc.at[source],
            send_sem=fsend.at[slot],
            recv_sem=frecv.at[source],
            device_id=(t, dest),
            device_id_type=MESH,
        )

    for d in range(1, K):
        score_copy(lax.rem(k + d, K), k, d).start()

    table_wait(S_MSG, m1, True)
    table_wait(S_REPLY, replies, True)
    table_wait(S_CAND, call, True)
    table_wait(S_SCORE, rr, True)
    for a, buf in ((A_OUT, wo_all), (A_K, wk_all), (A_V, wv_all), (A_CQ, wcq_all), (A_CO, wco_all), (A_MLP, wm_all)):
        relay_drain(a, buf)
    gather_drain(A_SCORE, ws_all)
    gather_drain(A_STATE, sall)
    pair_copy(0, wperm, core).wait_send()
    pair_copy(1, gains, core).wait_send()
    for n in range(1, K):
        normed_copy(others(n), k).wait_send()
        gated_copy(others(n), k).wait_send()
    for d in range(1, K):
        score_copy(lax.rem(k + d, K), k, d).wait_send()
    for d in range(1, K):
        source = lax.rem(k + K - d, K)
        score_copy(source, source, d).wait_recv()
    final = sc[0]
    for n in range(1, K):
        final += sc[n]
    scores_ref[...] = final


def body(
    T,
    K,
    table_rows,
    hist_owner,
    hist_row,
    ln_gain,
    w_proj,
    norm_gain,
    w_out,
    w_ckv,
    candidates,
    cand_group,
    cand_member,
    block_mask,
    w_cq,
    w_co,
    w_mlp,
    w_score,
):
    slab = table_rows.shape[0]
    cap = max(1, 2 * hist_owner.size // T)
    rows, hist = 16 * T, 64 * K
    tile = min(rows, 256)
    vmem, hbm = pl.BlockSpec(memory_space=pltpu.VMEM), pl.BlockSpec(memory_space=pltpu.HBM)
    scratch = [
        pltpu.SMEM((4,), I32),
        pltpu.SMEM((4,), I32),
        pltpu.SMEM((4, 4), I32),
        pltpu.VMEM((2, 64), I32),
        pltpu.VMEM((2, 64), I32),
        pltpu.VMEM((1, 256), F32),
        pltpu.VMEM((256, 2, 256), BF),
        pltpu.VMEM((2, 64), F32),
        pltpu.VMEM((256, 2, 128), BF),
        pltpu.VMEM((64 * K, 256), BF),
        pltpu.VMEM((1, 128), BF),
        pltpu.VMEM((slab, 256), BF),
        pltpu.VMEM((2, 128), I32),
        pltpu.VMEM((T, 2, 128), I32),
        pltpu.VMEM((T, 2 * cap, 128), BF),
        pltpu.VMEM((T, 2 * cap, 128), BF),
        pltpu.VMEM((T, 16, 256), BF),
        pltpu.VMEM((T, 16, 256), BF),
        pltpu.VMEM((2, 256, 512), BF),
        pltpu.VMEM((2, 1, 128), F32),
        pltpu.VMEM((K, 128, 256), BF),
        pltpu.VMEM((K, 128, 256), BF),
        pltpu.VMEM((K, 256, 128), BF),
        pltpu.VMEM((K, 128, 256), BF),
        pltpu.VMEM((K, 128, 256), BF),
        pltpu.VMEM((K, 256, 128), BF),
        pltpu.VMEM((K, 8, 128), F32),
        pltpu.VMEM((128, 256), F32),
        pltpu.VMEM((2, 64, 256), BF),
        pltpu.VMEM((K, 64, 256), BF),
        pltpu.VMEM((2, hist, 128), BF),
        pltpu.VMEM((2, hist, 128), BF),
        pltpu.VMEM((2, hist, 128), BF),
        pltpu.VMEM((2, hist, 128), BF),
        pltpu.VMEM((K, 64, 256), BF),
        pltpu.VMEM((2, K // 2, 64, 256), BF),
        pltpu.VMEM((K, 128, 256), BF),
        pltpu.VMEM((K, rows // tile, 2 * tile, 256), BF),
        pltpu.VMEM((K, 256, hist), BF),
        pltpu.VMEM((K, hist, 256), BF),
        pltpu.VMEM((rows, hist), BF),
        pltpu.VMEM((rows, 128), F32),
        pltpu.VMEM((T, 1, 128), F32),
        pltpu.VMEM((T, 1, 128), F32),
        pltpu.VMEM((K, 4, 128), F32),
        pltpu.SemaphoreType.DMA((16,)),
        pltpu.SemaphoreType.DMA((4, T)),
        pltpu.SemaphoreType.DMA((4, T)),
        pltpu.SemaphoreType.DMA((8, K)),
        pltpu.SemaphoreType.DMA((8, K)),
        pltpu.SemaphoreType.DMA((8, 2)),
        pltpu.SemaphoreType.DMA((2,)),
        pltpu.SemaphoreType.DMA((2,)),
        pltpu.SemaphoreType.DMA((K,)),
        pltpu.SemaphoreType.DMA((K,)),
        pltpu.SemaphoreType.DMA((K,)),
        pltpu.SemaphoreType.DMA((K,)),
        pltpu.SemaphoreType.DMA((K,)),
        pltpu.SemaphoreType.DMA((K,)),
    ]
    states, scores = pl.pallas_call(
        functools.partial(kernel, T, K, slab, cap),
        out_shape=(
            jax.ShapeDtypeStruct((2, 64, 256), BF),
            jax.ShapeDtypeStruct((4, 128), F32),
        ),
        in_specs=[hbm] * 16,
        out_specs=(vmem, vmem),
        scratch_shapes=scratch,
        compiler_params=pltpu.CompilerParams(
            collective_id=0, has_side_effects=True, vmem_limit_bytes=60 * 1024 * 1024
        ),
    )(
        cand_group,
        cand_member,
        block_mask,
        hist_owner,
        hist_row,
        ln_gain.reshape(1, 256),
        w_proj,
        norm_gain,
        w_ckv,
        candidates,
        w_score.reshape(1, 128),
        table_rows,
        w_out.reshape(128, 256),
        jnp.transpose(w_cq, (1, 2, 0)).reshape(128, 256),
        w_co.reshape(128, 256),
        w_mlp,
    )
    return states, scores[:, : 16 * K].reshape(4 * 16 * K)


def solution(mesh):
    T, K = mesh.shape["table"], mesh.shape["tensor"]
    return jax.shard_map(
        functools.partial(body, T, K),
        mesh=mesh,
        in_specs=(
            P("table", None),
            P("table", "tensor"),
            P("table", "tensor"),
            P(),
            P(None, "tensor", None),
            P("tensor", None),
            P("tensor", None, None),
            P(None, "tensor", None),
            P("table", None),
            P("table"),
            P("table"),
            P("table", None),
            P(None, "tensor", None),
            P("tensor", None, None),
            P(None, "tensor"),
            P("tensor"),
        ),
        out_specs=(P("table", "tensor", None), P("table")),
        check_vma=False,
    )
```

```python
import functools
import math

import jax
import jax.numpy as jnp
from jax import lax
from jax.experimental import pallas as pl
from jax.experimental.pallas import tpu as pltpu
from jax.sharding import PartitionSpec as P

MESH = pl.DeviceIdType.MESH
F32, BF, I32 = jnp.float32, jnp.bfloat16, jnp.int32
A_OUT, A_K, A_V, A_CQ, A_CO, A_MLP, A_SCORE, A_STATE = range(8)
S_MSG, S_REPLY, S_CAND, S_SCORE = range(4)


def dot(a, b):
    return lax.dot_general(a, b, (((1,), (0,)), ((), ())), preferred_element_type=F32)


def dot_nt(a, b):
    return lax.dot_general(a, b, (((1,), (1,)), ((), ())), preferred_element_type=F32)


def iota(shape, axis):
    return lax.broadcasted_iota(I32, shape, axis)


def silu_of_double(half):
    return half + half * jnp.tanh(half)


def kernel(
    T,
    K,
    SLAB,
    CAP,
    group_hbm,
    member_hbm,
    mask_hbm,
    owner_hbm,
    row_hbm,
    lngain_hbm,
    wproj_hbm,
    ngain_hbm,
    wckv_hbm,
    cand_hbm,
    wscore_hbm,
    table_hbm,
    wout_hbm,
    wcq_hbm,
    wco_hbm,
    wmlp_hbm,
    states_ref,
    scores_ref,
    group_s,
    member_s,
    mask_s,
    owner_ref,
    row_ref,
    lngain_ref,
    wproj_ref,
    ngain_ref,
    wckv_ref,
    cand_ref,
    wscore_ref,
    tab,
    msg,
    m1,
    rep,
    replies,
    csend,
    call,
    wperm,
    gains,
    wo_all,
    wk_all,
    wv_all,
    wcq_all,
    wco_all,
    wm_all,
    ws_all,
    hist_scr,
    nown,
    nall,
    pg,
    pv,
    pq,
    pk,
    gs,
    gall,
    sall,
    q2,
    k2,
    v2,
    mb,
    um,
    sr,
    rr,
    lsem,
    tsend,
    trecv,
    asend,
    arecv,
    hrecv,
    psend,
    precv,
    nsend,
    nrecv,
    gsend,
    grecv,
):
    t, k = lax.axis_index("table"), lax.axis_index("tensor")
    X = K // 2
    x, core = k // 2, k % 2
    sib = k + 1 - 2 * core
    HIST = 64 * K
    SL = T // K
    CB = 16 * K
    R = SL * CB
    home = t // SL
    TR = min(R, 256)
    NT = R // TR
    SLOTS = TR // CB
    SHIFT = SLAB.bit_length() - 1
    assert T == SL * K

    def local(i, src, dst):
        return pltpu.make_async_copy(src, dst, lsem.at[i])

    locals_ = [
        local(0, table_hbm, tab),
        local(1, wout_hbm, wo_all.at[k]),
        local(2, wcq_hbm, wcq_all.at[k]),
        local(3, wco_hbm, wco_all.at[k]),
        local(4, wmlp_hbm, wm_all.at[k]),
    ]
    ids_in = [
        local(5, owner_hbm, owner_ref),
        local(6, row_hbm, row_ref),
        local(7, group_hbm, group_s),
        local(8, member_hbm, member_s),
        local(9, mask_hbm, mask_s),
    ]
    weights_in = [
        local(10, wckv_hbm, wckv_ref),
        local(11, wproj_hbm, wproj_ref),
        local(12, wscore_hbm, wscore_ref),
        local(15, ngain_hbm, ngain_ref),
    ]
    late_in = [
        local(13, cand_hbm, cand_ref),
        local(14, lngain_hbm, lngain_ref),
    ]
    for c in ids_in + weights_in + locals_ + late_in:
        c.start()

    barrier = pltpu.get_barrier_semaphore()

    def greet(d, carry):
        pl.semaphore_signal(barrier, inc=1, device_id=(lax.rem(t + d, T), k), device_id_type=MESH)
        return carry

    lax.fori_loop(1, T, greet, 0)

    def greet_home(g, carry):
        @pl.when((g != t) | (k != home))
        def _():
            pl.semaphore_signal(barrier, inc=1, device_id=(g, home), device_id_type=MESH)

        return carry

    lax.fori_loop(0, T, greet_home, 0)
    for d in range(1, K):
        pl.semaphore_signal(barrier, inc=1, device_id=(t, lax.rem(k + d, K)), device_id_type=MESH)

    def over_table(stage, src_of, buf):
        def one(d, carry):
            peer = lax.rem(t + d, T)
            pltpu.make_async_remote_copy(
                src_ref=src_of(peer),
                dst_ref=buf.at[t],
                send_sem=tsend.at[stage, peer],
                recv_sem=trecv.at[stage, t],
                device_id=(peer, k),
                device_id_type=MESH,
            ).start()
            return carry

        lax.fori_loop(1, T, one, 0)

    def table_wait(stage, buf, sends):
        def one(d, carry):
            peer = lax.rem(t + T - d, T)
            copy = pltpu.make_async_remote_copy(
                src_ref=buf.at[peer],
                dst_ref=buf.at[peer],
                send_sem=tsend.at[stage, peer],
                recv_sem=trecv.at[stage, peer],
                device_id=(peer, k),
                device_id_type=MESH,
            )
            if sends:
                copy.wait_send()
            else:
                copy.wait_recv()
            return carry

        lax.fori_loop(1, T, one, 0)

    order = sorted(range(1, X), key=lambda d: min(d, X - d))

    def gather_copy(a, src, buf, chunk, slot, dest):
        return pltpu.make_async_remote_copy(
            src_ref=src,
            dst_ref=buf.at[chunk],
            send_sem=asend.at[a, slot],
            recv_sem=arecv.at[a, chunk],
            device_id=(t, dest),
            device_id_type=MESH,
        )

    def gather_start(a, src, buf):
        for n, d in enumerate(order):
            gather_copy(a, src, buf, k, n, lax.rem(x + d, X) * 2 + core).start()
        gather_copy(a, src, buf, k, X - 1, sib).start()

    def gather_recv(a, buf, chunk):
        gather_copy(a, buf.at[chunk], buf, chunk, 0, sib).wait_recv()

    def near(n):
        return lax.rem(x + X - order[n], X) * 2 + core

    def far(n):
        return lax.rem(x + X - order[n], X) * 2 + 1 - core

    def gather_pass(a, buf, n):
        chunk = near(n)
        gather_recv(a, buf, chunk)
        gather_copy(a, buf.at[chunk], buf, chunk, X + n, sib).start()

    def gather_rest(a, buf):
        gather_recv(a, buf, sib)
        for n in range(X - 1):
            gather_recv(a, buf, far(n))

    def gather_drain(a, buf):
        for slot in range(2 * X - 1):
            gather_copy(a, buf.at[k], buf, k, slot, sib).wait_send()

    assert X == 4
    right, left = lax.rem(x + 1, X) * 2 + core, lax.rem(x + X - 1, X) * 2 + core
    across = lax.rem(x + 2, X) * 2 + core

    def half_copy(a, buf, chunk, side, dest):
        size = buf.shape[1] // 2
        part = buf.at[chunk, pl.ds(side * size, size)]
        return pltpu.make_async_remote_copy(
            src_ref=part,
            dst_ref=part,
            send_sem=asend.at[a, 3 + side],
            recv_sem=hrecv.at[a, side],
            device_id=(t, dest),
            device_id_type=MESH,
        )

    def relay_start(a, src, buf):
        gather_copy(a, src, buf, k, 0, right).start()
        gather_copy(a, src, buf, k, 1, left).start()
        gather_copy(a, src, buf, k, 2, sib).start()

    def relay_pass(a, buf):
        gather_recv(a, buf, left)
        half_copy(a, buf, left, 0, right).start()
        gather_copy(a, buf.at[left], buf, left, 5, sib).start()
        gather_recv(a, buf, right)
        half_copy(a, buf, right, 1, left).start()
        gather_copy(a, buf.at[right], buf, right, 6, sib).start()

    def relay_finish(a, buf):
        half_copy(a, buf, across, 0, sib).wait_recv()
        half_copy(a, buf, across, 1, sib).wait_recv()
        gather_copy(a, buf.at[across], buf, across, 7, sib).start()

    def relay_drain(a, buf):
        for slot in (0, 1, 2, 5, 6, 7):
            gather_copy(a, buf.at[k], buf, k, slot, sib).wait_send()
        half_copy(a, buf, left, 0, right).wait_send()
        half_copy(a, buf, right, 1, left).wait_send()

    def pair_copy(n, buf, slot):
        return pltpu.make_async_remote_copy(
            src_ref=buf.at[slot],
            dst_ref=buf.at[slot],
            send_sem=psend.at[n],
            recv_sem=precv.at[n],
            device_id=(t, sib),
            device_id_type=MESH,
        )

    for c in ids_in:
        c.wait()
    ids = owner_ref[...] * SLAB + row_ref[...]
    own_row = jnp.concatenate([ids[0:1], ids[1:2]], axis=1)
    lane1 = iota((1, 128), 1)
    meta = jnp.zeros((1, 128), I32)
    for b in range(4):
        meta = jnp.where(lane1 == b, group_s[b], meta)
        meta = jnp.where(lane1 == 4 + b, member_s[b], meta)
        for q in range(4):
            meta = jnp.where(lane1 == 8 + 4 * b + q, mask_s[b, q], meta)
    msg[0:1, :] = own_row
    msg[1:2, :] = meta
    m1[t] = msg[...]

    pl.semaphore_wait(barrier, T - 1 + K - 1 + T - 1 + (k != home).astype(I32))
    over_table(S_MSG, lambda peer: msg, m1)

    relay_start(A_OUT, wout_hbm, wo_all)
    for c in weights_in:
        c.wait()
    wckv = wckv_ref[...]
    kv0, kv1 = wckv[:, 0, :], wckv[:, 1, :]
    wk_all[k] = jnp.concatenate([kv0[:, :64], kv1[:, :64]], axis=1).T
    wv_all[k] = jnp.concatenate([kv0[:, 64:], kv1[:, 64:]], axis=1)
    relay_start(A_K, wk_all.at[k], wk_all)
    relay_start(A_V, wv_all.at[k], wv_all)
    wproj = wproj_ref[...]
    w0, w1 = wproj[:, 0, :], wproj[:, 1, :]
    half_w = [w[:, 64 * i : 64 * i + 64] for i in range(4) for w in (w0, w1)]
    wperm[core] = jnp.concatenate(half_w, axis=1) * 0.5
    gains[core] = jnp.concatenate([ngain_ref[0:1, :], ngain_ref[1:2, :]], axis=1)
    pair_copy(0, wperm, core).start()
    pair_copy(1, gains, core).start()
    ws_all[k] = jnp.broadcast_to(wscore_ref[...].astype(F32).reshape(1, 128), (8, 128))

    upper = (iota((128, 128), 0) < iota((128, 128), 1)).astype(BF)
    own_slab = own_row >> SHIFT
    hot = iota((T, 128), 0) == own_slab
    rank = dot(hot.astype(BF), upper)
    slot_row = jnp.sum(jnp.where(hot, rank, 0.0), axis=0, keepdims=True) + own_slab.astype(F32) * (2 * CAP)
    eye = iota((128, 128), 0) == iota((128, 128), 1)
    slot_col = jnp.sum(jnp.where(eye, slot_row, 0.0), axis=1, keepdims=True).astype(I32)
    spots = iota((128, 2 * CAP * T), 1)
    pick_left = (spots == slot_col).astype(BF)
    pick_right = (spots == slot_col + CAP).astype(BF)

    table_wait(S_MSG, m1, False)
    relay_start(A_CQ, wcq_hbm, wcq_all)
    relay_start(A_CO, wco_hbm, wco_all)
    relay_start(A_MLP, wmlp_hbm, wm_all)
    gather_start(A_SCORE, ws_all.at[k], ws_all)
    wanted_ids = m1[:, 0, :]
    mine = (wanted_ids >> SHIFT) == t
    rank_in = dot(mine.astype(BF), upper)
    low = (wanted_ids & (SLAB - 1)).astype(F32)
    lane_t = iota((T, 128), 1)
    want = jnp.zeros((T, 128), F32)
    for r in range(CAP):
        of_r = jnp.sum(jnp.where(mine & (rank_in == r), low, 0.0), axis=1, keepdims=True)
        want = jnp.where(lane_t == r, of_r, want)
    want_i = want.astype(I32)
    spread = (iota((T * CAP, T), 0) // CAP == iota((T * CAP, T), 1)).astype(BF)
    high = dot(spread, (want_i >> 6).astype(F32).astype(BF))
    lower = dot(spread, (want_i & 63).astype(F32).astype(BF))
    in_lane = iota((T * CAP, 128), 1) == iota((T * CAP, 128), 0) % CAP
    want_col = jnp.sum(jnp.where(in_lane, high * 64.0 + lower, 0.0), axis=1, keepdims=True).astype(I32)
    locals_[0].wait()
    CH = min(512, SLAB)
    rows = jnp.zeros((T * CAP, 256), F32)
    at = iota((T * CAP, CH), 1)
    for c in range(SLAB // CH):
        rows += dot((at == want_col - c * CH).astype(BF), tab[c * CH : (c + 1) * CH, :])
    halves = [rows[:, :128].reshape(T, CAP, 128), rows[:, 128:].reshape(T, CAP, 128)]
    rep[...] = jnp.concatenate(halves, axis=1).astype(BF)
    replies[t] = rep[t]
    over_table(S_REPLY, lambda peer: rep.at[peer], replies)

    relay_pass(A_OUT, wo_all)
    relay_pass(A_K, wk_all)
    relay_pass(A_V, wv_all)

    for c in late_in:
        c.wait()

    @pl.when(k == home)
    def _():
        blocks = [cand_ref[b * CB : (b + 1) * CB, :] for b in range(4)]

        def fill(g, carry):
            block = jnp.zeros((CB, 256), BF)
            for b in range(4):
                block = jnp.where(group_s[b] == g, blocks[b], block)
            csend[g] = block
            return carry

        lax.fori_loop(0, T, fill, 0)
        call[t - SL * k] = csend[t]

    def cand_copy(peer, source):
        return pltpu.make_async_remote_copy(
            src_ref=csend.at[peer],
            dst_ref=call.at[source - SL * k],
            send_sem=tsend.at[S_CAND, peer],
            recv_sem=trecv.at[S_CAND, source],
            device_id=(peer, k),
            device_id_type=MESH,
        )

    def cand_all(action):
        @pl.when(k == home)
        def _():
            def one(d, carry):
                action(cand_copy(lax.rem(t + d, T), t))
                return carry

            lax.fori_loop(1, T, one, 0)

    metas = m1[pl.ds(SL * k, SL), 1, :].astype(F32)
    lane_s = iota((SL, 128), 1)

    def meta_lane(n):
        return jnp.sum(jnp.where(lane_s == n, metas, 0.0), axis=1, keepdims=True)

    here = [(meta_lane(b) == t.astype(F32)).astype(F32) for b in range(4)]
    member = sum(here[b] * meta_lane(4 + b) for b in range(4))
    reads = [sum(here[b] * meta_lane(8 + 4 * b + q) for b in range(4)) for q in range(4)]
    part = (iota((SL, HIST), 1) % (HIST // 2)) // (HIST // 8)
    reads_wide = jnp.zeros((SL, HIST), F32)
    for q in range(4):
        reads_wide = jnp.where(part == q, reads[q], reads_wide)
    for i in range(SL):
        um[i * CB : (i + 1) * CB, :] = jnp.broadcast_to(member[i : i + 1], (CB, 128))
        mb[i * CB : (i + 1) * CB, :] = jnp.broadcast_to(reads_wide[i : i + 1], (CB, HIST)).astype(BF)

    table_wait(S_REPLY, replies, False)
    got = replies[...].reshape(T * 2 * CAP, 128)
    history = jnp.concatenate([dot(pick_left, got), dot(pick_right, got)], axis=1)
    hist_scr[...] = history
    centred = history - jnp.mean(history, axis=1, keepdims=True)
    spread_v = jnp.mean(centred * centred, axis=1, keepdims=True)
    normed = (centred * lax.rsqrt(spread_v + 1e-5) * lngain_ref[...]).astype(BF)
    nown[0] = normed[:64]
    nown[1] = normed[64:]

    def normed_copy(dest, source):
        return pltpu.make_async_remote_copy(
            src_ref=nown.at[dest % 2],
            dst_ref=nall.at[source],
            send_sem=nsend.at[dest],
            recv_sem=nrecv.at[source],
            device_id=(t, dest),
            device_id_type=MESH,
        )

    def others(n):
        return lax.rem(k + n, K)

    for n in range(1, K):
        normed_copy(others(n), k).start()
    nall[k] = nown[core]
    cand_all(lambda copy: copy.start())
    pair_copy(0, wperm, 1 - core).wait_recv()
    pair_copy(1, gains, 1 - core).wait_recv()

    first = iota((128, 128), 1) < 64
    same_half = jnp.where((iota((128, 128), 0) < 64) == first, 1.0 / 64, 0.0).astype(BF)

    def project(chip):
        rows_n = nall[pl.ds(2 * chip, 2)].reshape(128, 256)
        place = pl.ds(pl.multiple_of(chip * 128, 128), 128)
        for p in range(2):
            out = silu_of_double(dot(rows_n, wperm[p])).astype(BF)
            values = out[:, 128:256]
            pv[p, place, :] = (values.astype(F32) - dot(values, same_half)).astype(BF)
            for n, ref in ((0, pg), (2, pq), (3, pk)):
                ref[p, place, :] = out[:, 128 * n : 128 * n + 128]

    normed_copy(sib, sib).wait_recv()
    project(x)
    for d in order:
        chip = lax.rem(x + d, X)
        for c in range(2):
            normed_copy(2 * chip + c, 2 * chip + c).wait_recv()
        project(chip)
    relay_finish(A_OUT, wo_all)
    relay_finish(A_K, wk_all)
    relay_finish(A_V, wv_all)
    relay_pass(A_CQ, wcq_all)
    relay_pass(A_CO, wco_all)
    relay_pass(A_MLP, wm_all)
    for n in range(X - 1):
        gather_pass(A_SCORE, ws_all, n)

    causal = (iota((256, 128), 0) & 127) >= iota((256, 128), 1)
    zero = jnp.zeros((128, 128), BF)

    def gated_copy(dest, source):
        return pltpu.make_async_remote_copy(
            src_ref=gs.at[dest],
            dst_ref=gall.at[source % 2, source // 2],
            send_sem=gsend.at[dest],
            recv_sem=grecv.at[source],
            device_id=(t, dest),
            device_id_type=MESH,
        )

    for group in ((0, 1), (2, 3)):
        for block in group:
            start = block * 128
            for p in range(2):
                queries = pq[p, start : start + 128, :] * 0.0625
                both = jnp.concatenate([jnp.where(first, queries, zero), jnp.where(first, zero, queries)], axis=0)
                half = dot_nt(both, pk[p, start : start + 128, :])
                weights = jnp.where(causal, silu_of_double(half), 0.0).astype(BF)
                total = dot(weights, pv[p, start : start + 128, :])
                if block:
                    weights = silu_of_double(dot_nt(both, pk[p, :start, :])).astype(BF)
                    total += dot(weights, pv[p, :start, :])
                off = jnp.where(first, total[:128], total[128:])
                spread_a = dot((off * off).astype(BF), same_half)
                gate = pg[p, start : start + 128, :].astype(F32)
                gated = (off * lax.rsqrt(spread_a + 1e-5) * gains[p] * gate).astype(BF)
                gs[2 * block, :, 128 * p : 128 * p + 128] = gated[:64]
                gs[2 * block + 1, :, 128 * p : 128 * p + 128] = gated[64:]
        for dest in [2 * block + half for block in group for half in range(2)]:

            @pl.when(k != dest)
            def _():
                gated_copy(dest, k).start()

    gall[core, x] = gs[k]

    relay_finish(A_CQ, wcq_all)
    for i in range(SL):

        @pl.when(SL * k + i != t)
        def _():
            cand_copy(t, SL * k + i).wait_recv()

    gather_rest(A_CQ, wcq_all)
    locals_[2].wait()
    first_r = iota((TR, 128), 1) < 64
    zero_r = jnp.zeros((TR, 128), BF)

    def make_queries(j, carry):
        for tile in range(NT):
            cands = call[tile * SLOTS : (tile + 1) * SLOTS].reshape(TR, 256)
            queries = dot_nt(cands, wcq_all[j]).astype(BF) * 0.0625
            one = um[tile * TR : (tile + 1) * TR, :] > 0.5
            parts = (jnp.where(one, zero_r, queries), jnp.where(one, queries, zero_r))
            q2[j, tile, :TR, :] = jnp.concatenate([jnp.where(first_r, q, zero_r) for q in parts], axis=1)
            q2[j, tile, TR:, :] = jnp.concatenate([jnp.where(first_r, zero_r, q) for q in parts], axis=1)
        return carry

    lax.fori_loop(0, K // 2, make_queries, 0)

    gather_rest(A_OUT, wo_all)
    locals_[1].wait()
    for n in range(1, K):
        gated_copy(others(n), others(n)).wait_recv()
    total = hist_scr[...]
    for m in range(X):
        pieces = jnp.concatenate([gall[0, m], gall[1, m]], axis=0)
        total += dot(pieces, wo_all[2 * m : 2 * m + 2].reshape(256, 256))
    states = total.astype(BF)
    sall[k] = states
    gather_start(A_STATE, sall.at[k], sall)
    states_ref[...] = states.reshape(2, 64, 256)
    relay_finish(A_CO, wco_all)
    relay_finish(A_MLP, wm_all)

    lax.fori_loop(K // 2, K, make_queries, 0)

    gather_rest(A_K, wk_all)
    gather_rest(A_V, wv_all)

    def make_kv(part, own):
        place = slice(part * (HIST // 2), (part + 1) * (HIST // 2))
        values_w = jnp.concatenate([wv_all[j] for j in range(K)], axis=1)
        for u in range(2):
            rows_s = jnp.concatenate([sall[2 * m + own, 64 * u : 64 * u + 64, :] for m in range(X)], axis=0)
            keys = dot_nt(wk_all[...].reshape(K * 128, 256), rows_s).astype(BF)
            values = dot(rows_s, values_w).astype(BF)
            for j in range(K):
                k2[j, 128 * u : 128 * u + 128, place] = keys[128 * j : 128 * j + 128]
                v2[j, place, 128 * u : 128 * u + 128] = values[:, 128 * j : 128 * j + 128]

    for n in range(X - 1):
        gather_pass(A_STATE, sall, n)
    make_kv(0, core)
    gather_rest(A_STATE, sall)
    make_kv(1, 1 - core)

    def cross_pair(j, tile):
        tile_rows = pl.ds(pl.multiple_of(tile * TR, TR), TR)
        reads_t = mb[tile_rows, :]
        weights = silu_of_double(dot(q2[j, tile], k2[j])).astype(BF)
        weights = jnp.concatenate([weights[:TR] * reads_t, weights[TR:] * reads_t], axis=0)
        out = dot(weights, v2[j])
        one = um[tile_rows, :] > 0.5
        top = jnp.where(one, out[:TR, 128:], out[:TR, :128])
        bottom = jnp.where(one, out[TR:, 128:], out[TR:, :128])
        return jnp.where(first_r, top, bottom)

    gather_rest(A_CO, wco_all)
    gather_rest(A_MLP, wm_all)
    gather_rest(A_SCORE, ws_all)
    locals_[3].wait()
    locals_[4].wait()
    at_lane = iota((TR, 128), 0) % CB == iota((TR, 128), 1)

    def finish_tile(tile, carry):
        mixed = call[pl.ds(tile * SLOTS, SLOTS)].reshape(TR, 256).astype(F32)
        for m in range(X):
            pair = [
                (cross_pair(j, tile) * (1.0 / math.sqrt(HIST))).astype(BF)
                for j in (2 * m, 2 * m + 1)
            ]
            mixed += dot(jnp.concatenate(pair, axis=1), wco_all[2 * m : 2 * m + 2].reshape(256, 256))
        mixed = mixed.astype(BF)
        total_s = jnp.zeros((TR, 128), F32)
        for m in range(X):
            half = dot(mixed, jnp.concatenate([wm_all[2 * m], wm_all[2 * m + 1]], axis=1)) * 0.5
            hidden = silu_of_double(half).astype(BF).astype(F32)
            total_s += hidden[:, :128] * ws_all[2 * m][0:1, :] + hidden[:, 128:] * ws_all[2 * m + 1][0:1, :]
        score = jnp.sum(total_s, axis=1, keepdims=True)
        by_slot = jnp.sum(jnp.where(at_lane, score, 0.0).reshape(SLOTS, CB, 128), axis=1)
        sr[pl.ds(tile * SLOTS, SLOTS)] = by_slot.reshape(SLOTS, 1, 128)
        for i in range(SLOTS):
            for j in range(K):
                score_send(tile * SLOTS + i, j, lambda copy: copy.start())
        return carry

    def score_copy(slot, j, source):
        return pltpu.make_async_remote_copy(
            src_ref=sr.at[slot],
            dst_ref=rr.at[source],
            send_sem=tsend.at[S_SCORE, slot * K + j],
            recv_sem=trecv.at[S_SCORE, source],
            device_id=(SL * k + slot, j),
            device_id_type=MESH,
        )

    def score_send(slot, j, action):
        @pl.when((SL * k + slot != t) | (j != k))
        def _():
            action(score_copy(slot, j, t))

    lax.fori_loop(0, NT, finish_tile, 0)

    @pl.when(k == home)
    def _():
        rr[t] = sr[t - SL * k]

    table_wait(S_MSG, m1, True)
    table_wait(S_REPLY, replies, True)
    cand_all(lambda copy: copy.wait_send())
    for a, buf in ((A_OUT, wo_all), (A_K, wk_all), (A_V, wv_all), (A_CQ, wcq_all), (A_CO, wco_all), (A_MLP, wm_all)):
        relay_drain(a, buf)
    gather_drain(A_SCORE, ws_all)
    gather_drain(A_STATE, sall)
    pair_copy(0, wperm, core).wait_send()
    pair_copy(1, gains, core).wait_send()
    for n in range(1, K):
        normed_copy(others(n), k).wait_send()
        gated_copy(others(n), k).wait_send()

    def score_wait(g, carry):
        @pl.when((g != t) | (k != home))
        def _():
            score_copy(0, 0, g).wait_recv()

        return carry

    lax.fori_loop(0, T, score_wait, 0)
    back = rr[...].reshape(T, 128)
    groups = iota((T, 128), 0)
    for b in range(4):
        scores_ref[b : b + 1, :] = jnp.sum(jnp.where(groups == group_s[b], back, 0.0), axis=0, keepdims=True)
    for slot in range(SL):
        for j in range(K):
            score_send(slot, j, lambda copy: copy.wait_send())


def body(
    T,
    K,
    table_rows,
    hist_owner,
    hist_row,
    ln_gain,
    w_proj,
    norm_gain,
    w_out,
    w_ckv,
    candidates,
    cand_group,
    cand_member,
    block_mask,
    w_cq,
    w_co,
    w_mlp,
    w_score,
):
    slab = table_rows.shape[0]
    cap = max(1, 2 * hist_owner.size // T)
    rows, hist = 16 * T, 64 * K
    tile = min(rows, 256)
    vmem, hbm = pl.BlockSpec(memory_space=pltpu.VMEM), pl.BlockSpec(memory_space=pltpu.HBM)
    scratch = [
        pltpu.SMEM((4,), I32),
        pltpu.SMEM((4,), I32),
        pltpu.SMEM((4, 4), I32),
        pltpu.VMEM((2, 64), I32),
        pltpu.VMEM((2, 64), I32),
        pltpu.VMEM((1, 256), F32),
        pltpu.VMEM((256, 2, 256), BF),
        pltpu.VMEM((2, 64), F32),
        pltpu.VMEM((256, 2, 128), BF),
        pltpu.VMEM((64 * K, 256), BF),
        pltpu.VMEM((1, 128), BF),
        pltpu.VMEM((slab, 256), BF),
        pltpu.VMEM((2, 128), I32),
        pltpu.VMEM((T, 2, 128), I32),
        pltpu.VMEM((T, 2 * cap, 128), BF),
        pltpu.VMEM((T, 2 * cap, 128), BF),
        pltpu.VMEM((T, 16 * K, 256), BF),
        pltpu.VMEM((T // K, 16 * K, 256), BF),
        pltpu.VMEM((2, 256, 512), BF),
        pltpu.VMEM((2, 1, 128), F32),
        pltpu.VMEM((K, 128, 256), BF),
        pltpu.VMEM((K, 128, 256), BF),
        pltpu.VMEM((K, 256, 128), BF),
        pltpu.VMEM((K, 128, 256), BF),
        pltpu.VMEM((K, 128, 256), BF),
        pltpu.VMEM((K, 256, 128), BF),
        pltpu.VMEM((K, 8, 128), F32),
        pltpu.VMEM((128, 256), F32),
        pltpu.VMEM((2, 64, 256), BF),
        pltpu.VMEM((K, 64, 256), BF),
        pltpu.VMEM((2, hist, 128), BF),
        pltpu.VMEM((2, hist, 128), BF),
        pltpu.VMEM((2, hist, 128), BF),
        pltpu.VMEM((2, hist, 128), BF),
        pltpu.VMEM((K, 64, 256), BF),
        pltpu.VMEM((2, K // 2, 64, 256), BF),
        pltpu.VMEM((K, 128, 256), BF),
        pltpu.VMEM((K, rows // tile, 2 * tile, 256), BF),
        pltpu.VMEM((K, 256, hist), BF),
        pltpu.VMEM((K, hist, 256), BF),
        pltpu.VMEM((rows, hist), BF),
        pltpu.VMEM((rows, 128), F32),
        pltpu.VMEM((T // K, 1, 128), F32),
        pltpu.VMEM((T, 1, 128), F32),
        pltpu.SemaphoreType.DMA((16,)),
        pltpu.SemaphoreType.DMA((4, T)),
        pltpu.SemaphoreType.DMA((4, T)),
        pltpu.SemaphoreType.DMA((8, K)),
        pltpu.SemaphoreType.DMA((8, K)),
        pltpu.SemaphoreType.DMA((8, 2)),
        pltpu.SemaphoreType.DMA((2,)),
        pltpu.SemaphoreType.DMA((2,)),
        pltpu.SemaphoreType.DMA((K,)),
        pltpu.SemaphoreType.DMA((K,)),
        pltpu.SemaphoreType.DMA((K,)),
        pltpu.SemaphoreType.DMA((K,)),
    ]
    states, scores = pl.pallas_call(
        functools.partial(kernel, T, K, slab, cap),
        out_shape=(
            jax.ShapeDtypeStruct((2, 64, 256), BF),
            jax.ShapeDtypeStruct((4, 128), F32),
        ),
        in_specs=[hbm] * 16,
        out_specs=(vmem, vmem),
        scratch_shapes=scratch,
        compiler_params=pltpu.CompilerParams(
            collective_id=0, has_side_effects=True, vmem_limit_bytes=60 * 1024 * 1024
        ),
    )(
        cand_group,
        cand_member,
        block_mask,
        hist_owner,
        hist_row,
        ln_gain.reshape(1, 256),
        w_proj,
        norm_gain,
        w_ckv,
        candidates,
        w_score.reshape(1, 128),
        table_rows,
        w_out.reshape(128, 256),
        jnp.transpose(w_cq, (1, 2, 0)).reshape(128, 256),
        w_co.reshape(128, 256),
        w_mlp,
    )
    return states, scores[:, : 16 * K].reshape(4 * 16 * K)


def solution(mesh):
    T, K = mesh.shape["table"], mesh.shape["tensor"]
    return jax.shard_map(
        functools.partial(body, T, K),
        mesh=mesh,
        in_specs=(
            P("table", None),
            P("table", "tensor"),
            P("table", "tensor"),
            P(),
            P(None, "tensor", None),
            P("tensor", None),
            P("tensor", None, None),
            P(None, "tensor", None),
            P("table", None),
            P("table"),
            P("table"),
            P("table", None),
            P(None, "tensor", None),
            P("tensor", None, None),
            P(None, "tensor"),
            P("tensor"),
        ),
        out_specs=(P("table", "tensor", None), P("table")),
        check_vma=False,
    )
```

```python
import functools
import math

import jax
import jax.numpy as jnp
from jax import lax
from jax.experimental import pallas as pl
from jax.experimental.pallas import tpu as pltpu
from jax.sharding import PartitionSpec as P

MESH = pl.DeviceIdType.MESH
F32, BF, I32 = jnp.float32, jnp.bfloat16, jnp.int32
A_OUT, A_K, A_V, A_CQ, A_CO, A_MLP, A_SCORE, A_STATE = range(8)
S_MSG, S_REPLY, S_CAND, S_SCORE = range(4)


def dot(a, b):
    return lax.dot_general(a, b, (((1,), (0,)), ((), ())), preferred_element_type=F32)


def dot_nt(a, b):
    return lax.dot_general(a, b, (((1,), (1,)), ((), ())), preferred_element_type=F32)


def iota(shape, axis):
    return lax.broadcasted_iota(I32, shape, axis)


def silu_of_double(half):
    return half + half * jnp.tanh(half)


def kernel(
    T,
    K,
    SLAB,
    CAP,
    group_hbm,
    member_hbm,
    mask_hbm,
    owner_hbm,
    row_hbm,
    lngain_hbm,
    wproj_hbm,
    ngain_hbm,
    wckv_hbm,
    cand_hbm,
    wscore_hbm,
    table_hbm,
    wout_hbm,
    wcq_hbm,
    wco_hbm,
    wmlp_hbm,
    states_ref,
    scores_ref,
    group_s,
    member_s,
    mask_s,
    owner_ref,
    row_ref,
    lngain_ref,
    wproj_ref,
    ngain_ref,
    wckv_ref,
    cand_ref,
    wscore_ref,
    tab,
    msg,
    m1,
    rep,
    replies,
    csend,
    cin,
    call,
    wperm,
    gains,
    wo_all,
    wk_all,
    wv_all,
    wcq_all,
    wco_all,
    wm_all,
    ws_all,
    hist_scr,
    nown,
    nall,
    pg,
    pv,
    pq,
    pk,
    gs,
    gall,
    sall,
    q2,
    k2,
    v2,
    mb,
    um,
    sr,
    rr,
    lsem,
    tsend,
    trecv,
    asend,
    arecv,
    hrecv,
    crecv,
    psend,
    precv,
    nsend,
    nrecv,
    gsend,
    grecv,
):
    t, k = lax.axis_index("table"), lax.axis_index("tensor")
    X = K // 2
    x, core = k // 2, k % 2
    sib = k + 1 - 2 * core
    HIST = 64 * K
    SL = T // K
    CB = 16 * K
    R = SL * CB
    home = t // SL
    TR = min(R, 256)
    NT = R // TR
    SLOTS = TR // CB
    SHIFT = SLAB.bit_length() - 1
    assert T == SL * K

    def local(i, src, dst):
        return pltpu.make_async_copy(src, dst, lsem.at[i])

    locals_ = [
        local(0, table_hbm, tab),
        local(1, wout_hbm, wo_all.at[k]),
        local(2, wcq_hbm, wcq_all.at[k]),
        local(3, wco_hbm, wco_all.at[k]),
        local(4, wmlp_hbm, wm_all.at[k]),
    ]
    ids_in = [
        local(5, owner_hbm, owner_ref),
        local(6, row_hbm, row_ref),
        local(7, group_hbm, group_s),
        local(8, member_hbm, member_s),
        local(9, mask_hbm, mask_s),
    ]
    weights_in = [
        local(10, wckv_hbm, wckv_ref),
        local(11, wproj_hbm, wproj_ref),
        local(12, wscore_hbm, wscore_ref),
        local(15, ngain_hbm, ngain_ref),
    ]
    late_in = [
        local(14, lngain_hbm, lngain_ref),
    ]
    cand_in = local(13, cand_hbm, cand_ref)
    for c in ids_in + weights_in + [cand_in] + locals_ + late_in:
        c.start()

    barrier = pltpu.get_barrier_semaphore()

    def greet(d, carry):
        pl.semaphore_signal(barrier, inc=1, device_id=(lax.rem(t + d, T), k), device_id_type=MESH)
        return carry

    lax.fori_loop(1, T, greet, 0)

    def greet_home(g, carry):
        @pl.when((g != t) | (k != home))
        def _():
            pl.semaphore_signal(barrier, inc=1, device_id=(g, home), device_id_type=MESH)

        return carry

    lax.fori_loop(0, T, greet_home, 0)
    for d in range(1, K):
        pl.semaphore_signal(barrier, inc=1, device_id=(t, lax.rem(k + d, K)), device_id_type=MESH)

    def over_table(stage, src_of, buf):
        def one(d, carry):
            peer = lax.rem(t + d, T)
            pltpu.make_async_remote_copy(
                src_ref=src_of(peer),
                dst_ref=buf.at[t],
                send_sem=tsend.at[stage, peer],
                recv_sem=trecv.at[stage, t],
                device_id=(peer, k),
                device_id_type=MESH,
            ).start()
            return carry

        lax.fori_loop(1, T, one, 0)

    def table_wait(stage, buf, sends):
        def one(d, carry):
            peer = lax.rem(t + T - d, T)
            copy = pltpu.make_async_remote_copy(
                src_ref=buf.at[peer],
                dst_ref=buf.at[peer],
                send_sem=tsend.at[stage, peer],
                recv_sem=trecv.at[stage, peer],
                device_id=(peer, k),
                device_id_type=MESH,
            )
            if sends:
                copy.wait_send()
            else:
                copy.wait_recv()
            return carry

        lax.fori_loop(1, T, one, 0)

    order = sorted(range(1, X), key=lambda d: min(d, X - d))

    def gather_copy(a, src, buf, chunk, slot, dest):
        return pltpu.make_async_remote_copy(
            src_ref=src,
            dst_ref=buf.at[chunk],
            send_sem=asend.at[a, slot],
            recv_sem=arecv.at[a, chunk],
            device_id=(t, dest),
            device_id_type=MESH,
        )

    def gather_start(a, src, buf):
        for n, d in enumerate(order):
            gather_copy(a, src, buf, k, n, lax.rem(x + d, X) * 2 + core).start()
        gather_copy(a, src, buf, k, X - 1, sib).start()

    def gather_recv(a, buf, chunk):
        gather_copy(a, buf.at[chunk], buf, chunk, 0, sib).wait_recv()

    def near(n):
        return lax.rem(x + X - order[n], X) * 2 + core

    def far(n):
        return lax.rem(x + X - order[n], X) * 2 + 1 - core

    def gather_pass(a, buf, n):
        chunk = near(n)
        gather_recv(a, buf, chunk)
        gather_copy(a, buf.at[chunk], buf, chunk, X + n, sib).start()

    def gather_rest(a, buf):
        gather_recv(a, buf, sib)
        for n in range(X - 1):
            gather_recv(a, buf, far(n))

    def gather_drain(a, buf):
        for slot in range(2 * X - 1):
            gather_copy(a, buf.at[k], buf, k, slot, sib).wait_send()

    assert X == 4
    right, left = lax.rem(x + 1, X) * 2 + core, lax.rem(x + X - 1, X) * 2 + core
    across = lax.rem(x + 2, X) * 2 + core

    def half_copy(a, buf, chunk, side, dest):
        size = buf.shape[1] // 2
        part = buf.at[chunk, pl.ds(side * size, size)]
        return pltpu.make_async_remote_copy(
            src_ref=part,
            dst_ref=part,
            send_sem=asend.at[a, 3 + side],
            recv_sem=hrecv.at[a, side],
            device_id=(t, dest),
            device_id_type=MESH,
        )

    def relay_start(a, src, buf):
        gather_copy(a, src, buf, k, 0, right).start()
        gather_copy(a, src, buf, k, 1, left).start()
        gather_copy(a, src, buf, k, 2, sib).start()

    def relay_pass(a, buf):
        gather_recv(a, buf, left)
        half_copy(a, buf, left, 0, right).start()
        gather_copy(a, buf.at[left], buf, left, 5, sib).start()
        gather_recv(a, buf, right)
        half_copy(a, buf, right, 1, left).start()
        gather_copy(a, buf.at[right], buf, right, 6, sib).start()

    def relay_finish(a, buf):
        half_copy(a, buf, across, 0, sib).wait_recv()
        half_copy(a, buf, across, 1, sib).wait_recv()
        gather_copy(a, buf.at[across], buf, across, 7, sib).start()

    def relay_drain(a, buf):
        for slot in (0, 1, 2, 5, 6, 7):
            gather_copy(a, buf.at[k], buf, k, slot, sib).wait_send()
        half_copy(a, buf, left, 0, right).wait_send()
        half_copy(a, buf, right, 1, left).wait_send()

    def pair_copy(n, buf, slot):
        return pltpu.make_async_remote_copy(
            src_ref=buf.at[slot],
            dst_ref=buf.at[slot],
            send_sem=psend.at[n],
            recv_sem=precv.at[n],
            device_id=(t, sib),
            device_id_type=MESH,
        )

    for c in ids_in:
        c.wait()
    ids = owner_ref[...] * SLAB + row_ref[...]
    own_row = jnp.concatenate([ids[0:1], ids[1:2]], axis=1)
    lane1 = iota((1, 128), 1)
    meta = jnp.zeros((1, 128), I32)
    for b in range(4):
        meta = jnp.where(lane1 == b, group_s[b], meta)
        meta = jnp.where(lane1 == 4 + b, member_s[b], meta)
        for q in range(4):
            meta = jnp.where(lane1 == 8 + 4 * b + q, mask_s[b, q], meta)
    msg[0:1, :] = own_row
    msg[1:2, :] = meta
    m1[t] = msg[...]

    pl.semaphore_wait(barrier, T - 1 + K - 1 + T - 1 + (k != home).astype(I32))
    over_table(S_MSG, lambda peer: msg, m1)

    relay_start(A_OUT, wout_hbm, wo_all)
    for c in weights_in:
        c.wait()
    wckv = wckv_ref[...]
    kv0, kv1 = wckv[:, 0, :], wckv[:, 1, :]
    wk_all[k] = jnp.concatenate([kv0[:, :64], kv1[:, :64]], axis=1).T
    wv_all[k] = jnp.concatenate([kv0[:, 64:], kv1[:, 64:]], axis=1)
    relay_start(A_K, wk_all.at[k], wk_all)
    relay_start(A_V, wv_all.at[k], wv_all)
    wproj = wproj_ref[...]
    w0, w1 = wproj[:, 0, :], wproj[:, 1, :]
    half_w = [w[:, 64 * i : 64 * i + 64] for i in range(4) for w in (w0, w1)]
    wperm[core] = jnp.concatenate(half_w, axis=1) * 0.5
    gains[core] = jnp.concatenate([ngain_ref[0:1, :], ngain_ref[1:2, :]], axis=1)
    pair_copy(0, wperm, core).start()
    pair_copy(1, gains, core).start()
    ws_all[k] = jnp.broadcast_to(wscore_ref[...].astype(F32).reshape(1, 128), (8, 128))

    cand_in.wait()
    mine_c = jnp.concatenate(
        [cand_ref[pl.ds(pl.multiple_of(b * CB + 16 * k, 16), 16), :] for b in range(4)], axis=0
    )
    row_c, col_c = iota((16 * T, 64), 0), iota((16 * T, 64), 1)
    col_group = jnp.zeros((16 * T, 64), I32)
    for b in range(4):
        col_group = jnp.where((col_c >> 4) == b, group_s[b], col_group)
    pick_c = ((row_c >> 4) == col_group) & ((row_c & 15) == (col_c & 15))
    csend[...] = dot(pick_c.astype(BF), mine_c).astype(BF).reshape(T, 16, 256)

    cin[t] = csend[t]
    over_table(S_CAND, lambda peer: csend.at[peer], cin)

    def cand_copy(dest, source):
        return pltpu.make_async_remote_copy(
            src_ref=cin.at[pl.ds(SL * dest, SL)],
            dst_ref=call.at[:, pl.ds(pl.multiple_of(16 * source, 16), 16)],
            send_sem=crecv.at[0, dest],
            recv_sem=crecv.at[1, source],
            device_id=(t, dest),
            device_id_type=MESH,
        )

    upper = (iota((128, 128), 0) < iota((128, 128), 1)).astype(BF)
    own_slab = own_row >> SHIFT
    hot = iota((T, 128), 0) == own_slab
    rank = dot(hot.astype(BF), upper)
    slot_row = jnp.sum(jnp.where(hot, rank, 0.0), axis=0, keepdims=True) + own_slab.astype(F32) * (2 * CAP)
    eye = iota((128, 128), 0) == iota((128, 128), 1)
    slot_col = jnp.sum(jnp.where(eye, slot_row, 0.0), axis=1, keepdims=True).astype(I32)
    spots = iota((128, 2 * CAP * T), 1)
    pick_left = (spots == slot_col).astype(BF)
    pick_right = (spots == slot_col + CAP).astype(BF)

    table_wait(S_MSG, m1, False)
    relay_start(A_CQ, wcq_hbm, wcq_all)
    relay_start(A_CO, wco_hbm, wco_all)
    relay_start(A_MLP, wmlp_hbm, wm_all)
    gather_start(A_SCORE, ws_all.at[k], ws_all)
    wanted_ids = m1[:, 0, :]
    mine = (wanted_ids >> SHIFT) == t
    rank_in = dot(mine.astype(BF), upper)
    low = (wanted_ids & (SLAB - 1)).astype(F32)
    lane_t = iota((T, 128), 1)
    want = jnp.zeros((T, 128), F32)
    for r in range(CAP):
        of_r = jnp.sum(jnp.where(mine & (rank_in == r), low, 0.0), axis=1, keepdims=True)
        want = jnp.where(lane_t == r, of_r, want)
    want_i = want.astype(I32)
    spread = (iota((T * CAP, T), 0) // CAP == iota((T * CAP, T), 1)).astype(BF)
    high = dot(spread, (want_i >> 6).astype(F32).astype(BF))
    lower = dot(spread, (want_i & 63).astype(F32).astype(BF))
    in_lane = iota((T * CAP, 128), 1) == iota((T * CAP, 128), 0) % CAP
    want_col = jnp.sum(jnp.where(in_lane, high * 64.0 + lower, 0.0), axis=1, keepdims=True).astype(I32)
    locals_[0].wait()
    CH = min(512, SLAB)
    rows = jnp.zeros((T * CAP, 256), F32)
    at = iota((T * CAP, CH), 1)
    for c in range(SLAB // CH):
        rows += dot((at == want_col - c * CH).astype(BF), tab[c * CH : (c + 1) * CH, :])
    halves = [rows[:, :128].reshape(T, CAP, 128), rows[:, 128:].reshape(T, CAP, 128)]
    rep[...] = jnp.concatenate(halves, axis=1).astype(BF)
    replies[t] = rep[t]
    over_table(S_REPLY, lambda peer: rep.at[peer], replies)

    relay_pass(A_OUT, wo_all)
    relay_pass(A_K, wk_all)
    relay_pass(A_V, wv_all)

    table_wait(S_CAND, cin, False)
    for n in range(1, K):
        cand_copy(lax.rem(k + n, K), k).start()
    call[:, pl.ds(pl.multiple_of(16 * k, 16), 16), :] = cin[pl.ds(SL * k, SL)]

    for c in late_in:
        c.wait()

    metas = m1[pl.ds(SL * k, SL), 1, :].astype(F32)
    lane_s = iota((SL, 128), 1)

    def meta_lane(n):
        return jnp.sum(jnp.where(lane_s == n, metas, 0.0), axis=1, keepdims=True)

    here = [(meta_lane(b) == t.astype(F32)).astype(F32) for b in range(4)]
    member = sum(here[b] * meta_lane(4 + b) for b in range(4))
    reads = [sum(here[b] * meta_lane(8 + 4 * b + q) for b in range(4)) for q in range(4)]
    part = (iota((SL, HIST), 1) % (HIST // 2)) // (HIST // 8)
    reads_wide = jnp.zeros((SL, HIST), F32)
    for q in range(4):
        reads_wide = jnp.where(part == q, reads[q], reads_wide)
    for i in range(SL):
        um[i * CB : (i + 1) * CB, :] = jnp.broadcast_to(member[i : i + 1], (CB, 128))
        mb[i * CB : (i + 1) * CB, :] = jnp.broadcast_to(reads_wide[i : i + 1], (CB, HIST)).astype(BF)

    table_wait(S_REPLY, replies, False)
    got = replies[...].reshape(T * 2 * CAP, 128)
    history = jnp.concatenate([dot(pick_left, got), dot(pick_right, got)], axis=1)
    hist_scr[...] = history
    centred = history - jnp.mean(history, axis=1, keepdims=True)
    spread_v = jnp.mean(centred * centred, axis=1, keepdims=True)
    normed = (centred * lax.rsqrt(spread_v + 1e-5) * lngain_ref[...]).astype(BF)
    nown[0] = normed[:64]
    nown[1] = normed[64:]

    def normed_copy(dest, source):
        return pltpu.make_async_remote_copy(
            src_ref=nown.at[dest % 2],
            dst_ref=nall.at[source],
            send_sem=nsend.at[dest],
            recv_sem=nrecv.at[source],
            device_id=(t, dest),
            device_id_type=MESH,
        )

    def others(n):
        return lax.rem(k + n, K)

    for n in range(1, K):
        normed_copy(others(n), k).start()
    nall[k] = nown[core]
    pair_copy(0, wperm, 1 - core).wait_recv()
    pair_copy(1, gains, 1 - core).wait_recv()

    first = iota((128, 128), 1) < 64
    same_half = jnp.where((iota((128, 128), 0) < 64) == first, 1.0 / 64, 0.0).astype(BF)

    def project(chip):
        rows_n = nall[pl.ds(2 * chip, 2)].reshape(128, 256)
        place = pl.ds(pl.multiple_of(chip * 128, 128), 128)
        for p in range(2):
            out = silu_of_double(dot(rows_n, wperm[p])).astype(BF)
            values = out[:, 128:256]
            pv[p, place, :] = (values.astype(F32) - dot(values, same_half)).astype(BF)
            for n, ref in ((0, pg), (2, pq), (3, pk)):
                ref[p, place, :] = out[:, 128 * n : 128 * n + 128]

    normed_copy(sib, sib).wait_recv()
    project(x)
    for d in order:
        chip = lax.rem(x + d, X)
        for c in range(2):
            normed_copy(2 * chip + c, 2 * chip + c).wait_recv()
        project(chip)
    relay_finish(A_OUT, wo_all)
    relay_finish(A_K, wk_all)
    relay_finish(A_V, wv_all)
    relay_pass(A_CQ, wcq_all)
    relay_pass(A_CO, wco_all)
    relay_pass(A_MLP, wm_all)
    for n in range(X - 1):
        gather_pass(A_SCORE, ws_all, n)

    causal = (iota((256, 128), 0) & 127) >= iota((256, 128), 1)
    zero = jnp.zeros((128, 128), BF)

    def gated_copy(dest, source):
        return pltpu.make_async_remote_copy(
            src_ref=gs.at[dest],
            dst_ref=gall.at[source % 2, source // 2],
            send_sem=gsend.at[dest],
            recv_sem=grecv.at[source],
            device_id=(t, dest),
            device_id_type=MESH,
        )

    for group in ((0, 1), (2, 3)):
        for block in group:
            start = block * 128
            for p in range(2):
                queries = pq[p, start : start + 128, :] * 0.0625
                both = jnp.concatenate([jnp.where(first, queries, zero), jnp.where(first, zero, queries)], axis=0)
                half = dot_nt(both, pk[p, start : start + 128, :])
                weights = jnp.where(causal, silu_of_double(half), 0.0).astype(BF)
                total = dot(weights, pv[p, start : start + 128, :])
                if block:
                    weights = silu_of_double(dot_nt(both, pk[p, :start, :])).astype(BF)
                    total += dot(weights, pv[p, :start, :])
                off = jnp.where(first, total[:128], total[128:])
                spread_a = dot((off * off).astype(BF), same_half)
                gate = pg[p, start : start + 128, :].astype(F32)
                gated = (off * lax.rsqrt(spread_a + 1e-5) * gains[p] * gate).astype(BF)
                gs[2 * block, :, 128 * p : 128 * p + 128] = gated[:64]
                gs[2 * block + 1, :, 128 * p : 128 * p + 128] = gated[64:]
        for dest in [2 * block + half for block in group for half in range(2)]:

            @pl.when(k != dest)
            def _():
                gated_copy(dest, k).start()

    gall[core, x] = gs[k]

    relay_finish(A_CQ, wcq_all)
    for n in range(1, K):
        cand_copy(others(n), others(n)).wait_recv()
    gather_rest(A_CQ, wcq_all)
    locals_[2].wait()
    first_r = iota((TR, 128), 1) < 64
    zero_r = jnp.zeros((TR, 128), BF)

    def make_queries(j, carry):
        for tile in range(NT):
            cands = call[tile * SLOTS : (tile + 1) * SLOTS].reshape(TR, 256)
            queries = dot_nt(cands, wcq_all[j]).astype(BF) * 0.0625
            one = um[tile * TR : (tile + 1) * TR, :] > 0.5
            parts = (jnp.where(one, zero_r, queries), jnp.where(one, queries, zero_r))
            q2[j, tile, :TR, :] = jnp.concatenate([jnp.where(first_r, q, zero_r) for q in parts], axis=1)
            q2[j, tile, TR:, :] = jnp.concatenate([jnp.where(first_r, zero_r, q) for q in parts], axis=1)
        return carry

    lax.fori_loop(0, K // 2, make_queries, 0)

    gather_rest(A_OUT, wo_all)
    locals_[1].wait()
    for n in range(1, K):
        gated_copy(others(n), others(n)).wait_recv()
    total = hist_scr[...]
    for m in range(X):
        pieces = jnp.concatenate([gall[0, m], gall[1, m]], axis=0)
        total += dot(pieces, wo_all[2 * m : 2 * m + 2].reshape(256, 256))
    states = total.astype(BF)
    sall[k] = states
    gather_start(A_STATE, sall.at[k], sall)
    states_ref[...] = states.reshape(2, 64, 256)
    relay_finish(A_CO, wco_all)
    relay_finish(A_MLP, wm_all)

    lax.fori_loop(K // 2, K, make_queries, 0)

    gather_rest(A_K, wk_all)
    gather_rest(A_V, wv_all)

    def make_kv(part, own):
        place = slice(part * (HIST // 2), (part + 1) * (HIST // 2))
        values_w = jnp.concatenate([wv_all[j] for j in range(K)], axis=1)
        for u in range(2):
            rows_s = jnp.concatenate([sall[2 * m + own, 64 * u : 64 * u + 64, :] for m in range(X)], axis=0)
            keys = dot_nt(wk_all[...].reshape(K * 128, 256), rows_s).astype(BF)
            values = dot(rows_s, values_w).astype(BF)
            for j in range(K):
                k2[j, 128 * u : 128 * u + 128, place] = keys[128 * j : 128 * j + 128]
                v2[j, place, 128 * u : 128 * u + 128] = values[:, 128 * j : 128 * j + 128]

    for n in range(X - 1):
        gather_pass(A_STATE, sall, n)
    make_kv(0, core)
    gather_rest(A_STATE, sall)
    make_kv(1, 1 - core)

    def cross_pair(j, tile):
        tile_rows = pl.ds(pl.multiple_of(tile * TR, TR), TR)
        reads_t = mb[tile_rows, :]
        weights = silu_of_double(dot(q2[j, tile], k2[j])).astype(BF)
        weights = jnp.concatenate([weights[:TR] * reads_t, weights[TR:] * reads_t], axis=0)
        out = dot(weights, v2[j])
        one = um[tile_rows, :] > 0.5
        top = jnp.where(one, out[:TR, 128:], out[:TR, :128])
        bottom = jnp.where(one, out[TR:, 128:], out[TR:, :128])
        return jnp.where(first_r, top, bottom)

    gather_rest(A_CO, wco_all)
    gather_rest(A_MLP, wm_all)
    gather_rest(A_SCORE, ws_all)
    locals_[3].wait()
    locals_[4].wait()
    at_lane = iota((TR, 128), 0) % CB == iota((TR, 128), 1)

    def finish_tile(tile, carry):
        mixed = call[pl.ds(tile * SLOTS, SLOTS)].reshape(TR, 256).astype(F32)
        for m in range(X):
            pair = [
                (cross_pair(j, tile) * (1.0 / math.sqrt(HIST))).astype(BF)
                for j in (2 * m, 2 * m + 1)
            ]
            mixed += dot(jnp.concatenate(pair, axis=1), wco_all[2 * m : 2 * m + 2].reshape(256, 256))
        mixed = mixed.astype(BF)
        total_s = jnp.zeros((TR, 128), F32)
        for m in range(X):
            half = dot(mixed, jnp.concatenate([wm_all[2 * m], wm_all[2 * m + 1]], axis=1)) * 0.5
            hidden = silu_of_double(half).astype(BF).astype(F32)
            total_s += hidden[:, :128] * ws_all[2 * m][0:1, :] + hidden[:, 128:] * ws_all[2 * m + 1][0:1, :]
        score = jnp.sum(total_s, axis=1, keepdims=True)
        by_slot = jnp.sum(jnp.where(at_lane, score, 0.0).reshape(SLOTS, CB, 128), axis=1)
        sr[pl.ds(tile * SLOTS, SLOTS)] = by_slot.reshape(SLOTS, 1, 128)
        for i in range(SLOTS):
            for j in range(K):
                score_send(tile * SLOTS + i, j, lambda copy: copy.start())
        return carry

    def score_copy(slot, j, source):
        return pltpu.make_async_remote_copy(
            src_ref=sr.at[slot],
            dst_ref=rr.at[source],
            send_sem=tsend.at[S_SCORE, slot * K + j],
            recv_sem=trecv.at[S_SCORE, source],
            device_id=(SL * k + slot, j),
            device_id_type=MESH,
        )

    def score_send(slot, j, action):
        @pl.when((SL * k + slot != t) | (j != k))
        def _():
            action(score_copy(slot, j, t))

    lax.fori_loop(0, NT, finish_tile, 0)

    @pl.when(k == home)
    def _():
        rr[t] = sr[t - SL * k]

    table_wait(S_MSG, m1, True)
    table_wait(S_REPLY, replies, True)
    table_wait(S_CAND, cin, True)
    for n in range(1, K):
        cand_copy(others(n), k).wait_send()
    for a, buf in ((A_OUT, wo_all), (A_K, wk_all), (A_V, wv_all), (A_CQ, wcq_all), (A_CO, wco_all), (A_MLP, wm_all)):
        relay_drain(a, buf)
    gather_drain(A_SCORE, ws_all)
    gather_drain(A_STATE, sall)
    pair_copy(0, wperm, core).wait_send()
    pair_copy(1, gains, core).wait_send()
    for n in range(1, K):
        normed_copy(others(n), k).wait_send()
        gated_copy(others(n), k).wait_send()

    def score_wait(g, carry):
        @pl.when((g != t) | (k != home))
        def _():
            score_copy(0, 0, g).wait_recv()

        return carry

    lax.fori_loop(0, T, score_wait, 0)
    back = rr[...].reshape(T, 128)
    groups = iota((T, 128), 0)
    for b in range(4):
        scores_ref[b : b + 1, :] = jnp.sum(jnp.where(groups == group_s[b], back, 0.0), axis=0, keepdims=True)
    for slot in range(SL):
        for j in range(K):
            score_send(slot, j, lambda copy: copy.wait_send())


def body(
    T,
    K,
    table_rows,
    hist_owner,
    hist_row,
    ln_gain,
    w_proj,
    norm_gain,
    w_out,
    w_ckv,
    candidates,
    cand_group,
    cand_member,
    block_mask,
    w_cq,
    w_co,
    w_mlp,
    w_score,
):
    slab = table_rows.shape[0]
    cap = max(1, 2 * hist_owner.size // T)
    rows, hist = 16 * T, 64 * K
    tile = min(rows, 256)
    vmem, hbm = pl.BlockSpec(memory_space=pltpu.VMEM), pl.BlockSpec(memory_space=pltpu.HBM)
    scratch = [
        pltpu.SMEM((4,), I32),
        pltpu.SMEM((4,), I32),
        pltpu.SMEM((4, 4), I32),
        pltpu.VMEM((2, 64), I32),
        pltpu.VMEM((2, 64), I32),
        pltpu.VMEM((1, 256), F32),
        pltpu.VMEM((256, 2, 256), BF),
        pltpu.VMEM((2, 64), F32),
        pltpu.VMEM((256, 2, 128), BF),
        pltpu.VMEM((64 * K, 256), BF),
        pltpu.VMEM((1, 128), BF),
        pltpu.VMEM((slab, 256), BF),
        pltpu.VMEM((2, 128), I32),
        pltpu.VMEM((T, 2, 128), I32),
        pltpu.VMEM((T, 2 * cap, 128), BF),
        pltpu.VMEM((T, 2 * cap, 128), BF),
        pltpu.VMEM((T, 16, 256), BF),
        pltpu.VMEM((T, 16, 256), BF),
        pltpu.VMEM((T // K, 16 * K, 256), BF),
        pltpu.VMEM((2, 256, 512), BF),
        pltpu.VMEM((2, 1, 128), F32),
        pltpu.VMEM((K, 128, 256), BF),
        pltpu.VMEM((K, 128, 256), BF),
        pltpu.VMEM((K, 256, 128), BF),
        pltpu.VMEM((K, 128, 256), BF),
        pltpu.VMEM((K, 128, 256), BF),
        pltpu.VMEM((K, 256, 128), BF),
        pltpu.VMEM((K, 8, 128), F32),
        pltpu.VMEM((128, 256), F32),
        pltpu.VMEM((2, 64, 256), BF),
        pltpu.VMEM((K, 64, 256), BF),
        pltpu.VMEM((2, hist, 128), BF),
        pltpu.VMEM((2, hist, 128), BF),
        pltpu.VMEM((2, hist, 128), BF),
        pltpu.VMEM((2, hist, 128), BF),
        pltpu.VMEM((K, 64, 256), BF),
        pltpu.VMEM((2, K // 2, 64, 256), BF),
        pltpu.VMEM((K, 128, 256), BF),
        pltpu.VMEM((K, rows // tile, 2 * tile, 256), BF),
        pltpu.VMEM((K, 256, hist), BF),
        pltpu.VMEM((K, hist, 256), BF),
        pltpu.VMEM((rows, hist), BF),
        pltpu.VMEM((rows, 128), F32),
        pltpu.VMEM((T // K, 1, 128), F32),
        pltpu.VMEM((T, 1, 128), F32),
        pltpu.SemaphoreType.DMA((16,)),
        pltpu.SemaphoreType.DMA((4, T)),
        pltpu.SemaphoreType.DMA((4, T)),
        pltpu.SemaphoreType.DMA((8, K)),
        pltpu.SemaphoreType.DMA((8, K)),
        pltpu.SemaphoreType.DMA((8, 2)),
        pltpu.SemaphoreType.DMA((2, K)),
        pltpu.SemaphoreType.DMA((2,)),
        pltpu.SemaphoreType.DMA((2,)),
        pltpu.SemaphoreType.DMA((K,)),
        pltpu.SemaphoreType.DMA((K,)),
        pltpu.SemaphoreType.DMA((K,)),
        pltpu.SemaphoreType.DMA((K,)),
    ]
    states, scores = pl.pallas_call(
        functools.partial(kernel, T, K, slab, cap),
        out_shape=(
            jax.ShapeDtypeStruct((2, 64, 256), BF),
            jax.ShapeDtypeStruct((4, 128), F32),
        ),
        in_specs=[hbm] * 16,
        out_specs=(vmem, vmem),
        scratch_shapes=scratch,
        compiler_params=pltpu.CompilerParams(
            collective_id=0, has_side_effects=True, vmem_limit_bytes=60 * 1024 * 1024
        ),
    )(
        cand_group,
        cand_member,
        block_mask,
        hist_owner,
        hist_row,
        ln_gain.reshape(1, 256),
        w_proj,
        norm_gain,
        w_ckv,
        candidates,
        w_score.reshape(1, 128),
        table_rows,
        w_out.reshape(128, 256),
        jnp.transpose(w_cq, (1, 2, 0)).reshape(128, 256),
        w_co.reshape(128, 256),
        w_mlp,
    )
    return states, scores[:, : 16 * K].reshape(4 * 16 * K)


def solution(mesh):
    T, K = mesh.shape["table"], mesh.shape["tensor"]
    return jax.shard_map(
        functools.partial(body, T, K),
        mesh=mesh,
        in_specs=(
            P("table", None),
            P("table", "tensor"),
            P("table", "tensor"),
            P(),
            P(None, "tensor", None),
            P("tensor", None),
            P("tensor", None, None),
            P(None, "tensor", None),
            P("table", None),
            P("table"),
            P("table"),
            P("table", None),
            P(None, "tensor", None),
            P("tensor", None, None),
            P(None, "tensor"),
            P("tensor"),
        ),
        out_specs=(P("table", "tensor", None), P("table")),
        check_vma=False,
    )
```

```python
import functools
import math

import jax
import jax.numpy as jnp
from jax import lax
from jax.experimental import pallas as pl
from jax.experimental.pallas import tpu as pltpu
from jax.sharding import PartitionSpec as P

MESH = pl.DeviceIdType.MESH
F32, BF, I32 = jnp.float32, jnp.bfloat16, jnp.int32
A_OUT, A_K, A_V, A_CQ, A_CO, A_MLP, A_SCORE, A_STATE = range(8)
S_MSG, S_REPLY, S_CAND, S_SCORE = range(4)


def dot(a, b):
    return lax.dot_general(a, b, (((1,), (0,)), ((), ())), preferred_element_type=F32)


def dot_nt(a, b):
    return lax.dot_general(a, b, (((1,), (1,)), ((), ())), preferred_element_type=F32)


def iota(shape, axis):
    return lax.broadcasted_iota(I32, shape, axis)


def silu_of_double(half):
    return half + half * jnp.tanh(half)


def kernel(
    T,
    K,
    SLAB,
    CAP,
    group_hbm,
    member_hbm,
    mask_hbm,
    owner_hbm,
    row_hbm,
    lngain_hbm,
    wproj_hbm,
    ngain_hbm,
    wckv_hbm,
    cand_hbm,
    wscore_hbm,
    table_hbm,
    wout_hbm,
    wcq_hbm,
    wco_hbm,
    wmlp_hbm,
    states_ref,
    scores_ref,
    group_s,
    member_s,
    mask_s,
    owner_ref,
    row_ref,
    lngain_ref,
    wproj_ref,
    ngain_ref,
    wckv_ref,
    cand_ref,
    wscore_ref,
    tab,
    msg,
    m1,
    rep,
    replies,
    csend,
    cin,
    call,
    wperm,
    gains,
    wo_all,
    wk_all,
    wv_all,
    wcq_all,
    wco_all,
    wm_all,
    ws_all,
    hist_scr,
    nown,
    nall,
    pg,
    pv,
    pq,
    pk,
    gs,
    gall,
    sall,
    q2,
    k2,
    v2,
    mb,
    um,
    sr,
    rr,
    lsem,
    tsend,
    trecv,
    asend,
    arecv,
    hrecv,
    crecv,
    psend,
    precv,
    nsend,
    nrecv,
    gsend,
    grecv,
):
    t, k = lax.axis_index("table"), lax.axis_index("tensor")
    X = K // 2
    x, core = k // 2, k % 2
    sib = k + 1 - 2 * core
    HIST = 64 * K
    SL = T // K
    CB = 16 * K
    R = SL * CB
    home = t // SL
    TR = min(R, 256)
    NT = R // TR
    SLOTS = TR // CB
    SHIFT = SLAB.bit_length() - 1
    assert T == SL * K

    def local(i, src, dst):
        return pltpu.make_async_copy(src, dst, lsem.at[i])

    locals_ = [
        local(0, table_hbm, tab),
        local(1, wout_hbm, wo_all.at[k]),
        local(2, wcq_hbm, wcq_all.at[k]),
        local(3, wco_hbm, wco_all.at[k]),
        local(4, wmlp_hbm, wm_all.at[k]),
    ]
    ids_in = [
        local(5, owner_hbm, owner_ref),
        local(6, row_hbm, row_ref),
        local(7, group_hbm, group_s),
        local(8, member_hbm, member_s),
        local(9, mask_hbm, mask_s),
    ]
    weights_in = [
        local(10, wckv_hbm, wckv_ref),
        local(11, wproj_hbm, wproj_ref),
        local(12, wscore_hbm, wscore_ref),
        local(15, ngain_hbm, ngain_ref),
    ]
    late_in = [
        local(14, lngain_hbm, lngain_ref),
    ]
    cand_in = local(13, cand_hbm, cand_ref)
    for c in ids_in + weights_in + [cand_in] + locals_ + late_in:
        c.start()

    barrier = pltpu.get_barrier_semaphore()

    def greet(d, carry):
        pl.semaphore_signal(barrier, inc=1, device_id=(lax.rem(t + d, T), k), device_id_type=MESH)
        return carry

    lax.fori_loop(1, T, greet, 0)

    def greet_home(g, carry):
        @pl.when((g != t) | (k != home))
        def _():
            pl.semaphore_signal(barrier, inc=1, device_id=(g, home), device_id_type=MESH)

        return carry

    lax.fori_loop(0, T, greet_home, 0)
    for d in range(1, K):
        pl.semaphore_signal(barrier, inc=1, device_id=(t, lax.rem(k + d, K)), device_id_type=MESH)

    def over_table(stage, src_of, buf):
        def one(d, carry):
            peer = lax.rem(t + d, T)
            pltpu.make_async_remote_copy(
                src_ref=src_of(peer),
                dst_ref=buf.at[t],
                send_sem=tsend.at[stage, peer],
                recv_sem=trecv.at[stage, t],
                device_id=(peer, k),
                device_id_type=MESH,
            ).start()
            return carry

        lax.fori_loop(1, T, one, 0)

    def table_wait(stage, buf, sends):
        def one(d, carry):
            peer = lax.rem(t + T - d, T)
            copy = pltpu.make_async_remote_copy(
                src_ref=buf.at[peer],
                dst_ref=buf.at[peer],
                send_sem=tsend.at[stage, peer],
                recv_sem=trecv.at[stage, peer],
                device_id=(peer, k),
                device_id_type=MESH,
            )
            if sends:
                copy.wait_send()
            else:
                copy.wait_recv()
            return carry

        lax.fori_loop(1, T, one, 0)

    order = sorted(range(1, X), key=lambda d: min(d, X - d))

    def gather_copy(a, src, buf, chunk, slot, dest):
        return pltpu.make_async_remote_copy(
            src_ref=src,
            dst_ref=buf.at[chunk],
            send_sem=asend.at[a, slot],
            recv_sem=arecv.at[a, chunk],
            device_id=(t, dest),
            device_id_type=MESH,
        )

    def gather_start(a, src, buf):
        for n, d in enumerate(order):
            gather_copy(a, src, buf, k, n, lax.rem(x + d, X) * 2 + core).start()
        gather_copy(a, src, buf, k, X - 1, sib).start()

    def gather_recv(a, buf, chunk):
        gather_copy(a, buf.at[chunk], buf, chunk, 0, sib).wait_recv()

    def near(n):
        return lax.rem(x + X - order[n], X) * 2 + core

    def far(n):
        return lax.rem(x + X - order[n], X) * 2 + 1 - core

    def gather_pass(a, buf, n):
        chunk = near(n)
        gather_recv(a, buf, chunk)
        gather_copy(a, buf.at[chunk], buf, chunk, X + n, sib).start()

    def gather_rest(a, buf):
        gather_recv(a, buf, sib)
        for n in range(X - 1):
            gather_recv(a, buf, far(n))

    def gather_drain(a, buf):
        for slot in range(2 * X - 1):
            gather_copy(a, buf.at[k], buf, k, slot, sib).wait_send()

    assert X == 4
    right, left = lax.rem(x + 1, X) * 2 + core, lax.rem(x + X - 1, X) * 2 + core
    across = lax.rem(x + 2, X) * 2 + core

    def half_copy(a, buf, chunk, side, dest):
        size = buf.shape[1] // 2
        part = buf.at[chunk, pl.ds(side * size, size)]
        return pltpu.make_async_remote_copy(
            src_ref=part,
            dst_ref=part,
            send_sem=asend.at[a, 3 + side],
            recv_sem=hrecv.at[a, side],
            device_id=(t, dest),
            device_id_type=MESH,
        )

    def relay_start(a, src, buf):
        gather_copy(a, src, buf, k, 0, right).start()
        gather_copy(a, src, buf, k, 1, left).start()
        gather_copy(a, src, buf, k, 2, sib).start()

    def relay_pass(a, buf):
        gather_recv(a, buf, left)
        half_copy(a, buf, left, 0, right).start()
        gather_copy(a, buf.at[left], buf, left, 5, sib).start()
        gather_recv(a, buf, right)
        half_copy(a, buf, right, 1, left).start()
        gather_copy(a, buf.at[right], buf, right, 6, sib).start()

    def relay_finish(a, buf):
        half_copy(a, buf, across, 0, sib).wait_recv()
        half_copy(a, buf, across, 1, sib).wait_recv()
        gather_copy(a, buf.at[across], buf, across, 7, sib).start()

    def relay_drain(a, buf):
        for slot in (0, 1, 2, 5, 6, 7):
            gather_copy(a, buf.at[k], buf, k, slot, sib).wait_send()
        half_copy(a, buf, left, 0, right).wait_send()
        half_copy(a, buf, right, 1, left).wait_send()

    def pair_copy(n, buf, slot):
        return pltpu.make_async_remote_copy(
            src_ref=buf.at[slot],
            dst_ref=buf.at[slot],
            send_sem=psend.at[n],
            recv_sem=precv.at[n],
            device_id=(t, sib),
            device_id_type=MESH,
        )

    for c in ids_in:
        c.wait()
    ids = owner_ref[...] * SLAB + row_ref[...]
    own_row = jnp.concatenate([ids[0:1], ids[1:2]], axis=1)
    lane1 = iota((1, 128), 1)
    meta = jnp.zeros((1, 128), I32)
    for b in range(4):
        meta = jnp.where(lane1 == b, group_s[b], meta)
        meta = jnp.where(lane1 == 4 + b, member_s[b], meta)
        for q in range(4):
            meta = jnp.where(lane1 == 8 + 4 * b + q, mask_s[b, q], meta)
    msg[0:1, :] = own_row
    msg[1:2, :] = meta
    m1[t] = msg[...]

    pl.semaphore_wait(barrier, T - 1 + K - 1 + T - 1 + (k != home).astype(I32))
    over_table(S_MSG, lambda peer: msg, m1)

    relay_start(A_OUT, wout_hbm, wo_all)
    for c in weights_in:
        c.wait()
    wckv = wckv_ref[...]
    kv0, kv1 = wckv[:, 0, :], wckv[:, 1, :]
    wk_all[k] = jnp.concatenate([kv0[:, :64], kv1[:, :64]], axis=1).T
    wv_all[k] = jnp.concatenate([kv0[:, 64:], kv1[:, 64:]], axis=1)
    relay_start(A_K, wk_all.at[k], wk_all)
    relay_start(A_V, wv_all.at[k], wv_all)
    relay_start(A_CQ, wcq_hbm, wcq_all)
    relay_start(A_CO, wco_hbm, wco_all)
    relay_start(A_MLP, wmlp_hbm, wm_all)
    wproj = wproj_ref[...]
    w0, w1 = wproj[:, 0, :], wproj[:, 1, :]
    half_w = [w[:, 64 * i : 64 * i + 64] for i in range(4) for w in (w0, w1)]
    wperm[core] = jnp.concatenate(half_w, axis=1) * 0.5
    gains[core] = jnp.concatenate([ngain_ref[0:1, :], ngain_ref[1:2, :]], axis=1)
    pair_copy(0, wperm, core).start()
    pair_copy(1, gains, core).start()
    ws_all[k] = jnp.broadcast_to(wscore_ref[...].astype(F32).reshape(1, 128), (8, 128))
    gather_start(A_SCORE, ws_all.at[k], ws_all)

    cand_in.wait()
    mine_c = jnp.concatenate(
        [cand_ref[pl.ds(pl.multiple_of(b * CB + 16 * k, 16), 16), :] for b in range(4)], axis=0
    )
    row_c, col_c = iota((16 * T, 64), 0), iota((16 * T, 64), 1)
    col_group = jnp.zeros((16 * T, 64), I32)
    for b in range(4):
        col_group = jnp.where((col_c >> 4) == b, group_s[b], col_group)
    pick_c = ((row_c >> 4) == col_group) & ((row_c & 15) == (col_c & 15))
    csend[...] = dot(pick_c.astype(BF), mine_c).astype(BF).reshape(T, 16, 256)

    cin[t] = csend[t]
    over_table(S_CAND, lambda peer: csend.at[peer], cin)

    def cand_copy(dest, source):
        return pltpu.make_async_remote_copy(
            src_ref=cin.at[pl.ds(SL * dest, SL)],
            dst_ref=call.at[:, pl.ds(pl.multiple_of(16 * source, 16), 16)],
            send_sem=crecv.at[0, dest],
            recv_sem=crecv.at[1, source],
            device_id=(t, dest),
            device_id_type=MESH,
        )

    upper = (iota((128, 128), 0) < iota((128, 128), 1)).astype(BF)
    own_slab = own_row >> SHIFT
    hot = iota((T, 128), 0) == own_slab
    rank = dot(hot.astype(BF), upper)
    slot_row = jnp.sum(jnp.where(hot, rank, 0.0), axis=0, keepdims=True) + own_slab.astype(F32) * (2 * CAP)
    eye = iota((128, 128), 0) == iota((128, 128), 1)
    slot_col = jnp.sum(jnp.where(eye, slot_row, 0.0), axis=1, keepdims=True).astype(I32)
    spots = iota((128, 2 * CAP * T), 1)
    pick_left = (spots == slot_col).astype(BF)
    pick_right = (spots == slot_col + CAP).astype(BF)

    table_wait(S_MSG, m1, False)
    wanted_ids = m1[:, 0, :]
    mine = (wanted_ids >> SHIFT) == t
    rank_in = dot(mine.astype(BF), upper)
    low = (wanted_ids & (SLAB - 1)).astype(F32)
    lane_t = iota((T, 128), 1)
    want = jnp.zeros((T, 128), F32)
    for r in range(CAP):
        of_r = jnp.sum(jnp.where(mine & (rank_in == r), low, 0.0), axis=1, keepdims=True)
        want = jnp.where(lane_t == r, of_r, want)
    want_i = want.astype(I32)
    spread = (iota((T * CAP, T), 0) // CAP == iota((T * CAP, T), 1)).astype(BF)
    high = dot(spread, (want_i >> 6).astype(F32).astype(BF))
    lower = dot(spread, (want_i & 63).astype(F32).astype(BF))
    in_lane = iota((T * CAP, 128), 1) == iota((T * CAP, 128), 0) % CAP
    want_col = jnp.sum(jnp.where(in_lane, high * 64.0 + lower, 0.0), axis=1, keepdims=True).astype(I32)
    locals_[0].wait()
    CH = min(512, SLAB)
    rows = jnp.zeros((T * CAP, 256), F32)
    in_chunk = (iota((T * CAP, CH), 1) == (want_col & (CH - 1))).astype(BF)
    of_chunk = want_col // CH
    for c in range(SLAB // CH):
        rows += jnp.where(of_chunk == c, dot(in_chunk, tab[c * CH : (c + 1) * CH, :]), 0.0)
    halves = [rows[:, :128].reshape(T, CAP, 128), rows[:, 128:].reshape(T, CAP, 128)]
    rep[...] = jnp.concatenate(halves, axis=1).astype(BF)
    replies[t] = rep[t]
    over_table(S_REPLY, lambda peer: rep.at[peer], replies)

    relay_pass(A_OUT, wo_all)
    relay_pass(A_K, wk_all)
    relay_pass(A_V, wv_all)

    table_wait(S_CAND, cin, False)
    for n in range(1, K):
        cand_copy(lax.rem(k + n, K), k).start()
    call[:, pl.ds(pl.multiple_of(16 * k, 16), 16), :] = cin[pl.ds(SL * k, SL)]

    for c in late_in:
        c.wait()

    metas = m1[pl.ds(SL * k, SL), 1, :].astype(F32)
    lane_s = iota((SL, 128), 1)

    def meta_lane(n):
        return jnp.sum(jnp.where(lane_s == n, metas, 0.0), axis=1, keepdims=True)

    here = [(meta_lane(b) == t.astype(F32)).astype(F32) for b in range(4)]
    member = sum(here[b] * meta_lane(4 + b) for b in range(4))
    reads = [sum(here[b] * meta_lane(8 + 4 * b + q) for b in range(4)) for q in range(4)]
    part = (iota((SL, HIST), 1) % (HIST // 2)) // (HIST // 8)
    reads_wide = jnp.zeros((SL, HIST), F32)
    for q in range(4):
        reads_wide = jnp.where(part == q, reads[q], reads_wide)
    for i in range(SL):
        um[i * CB : (i + 1) * CB, :] = jnp.broadcast_to(member[i : i + 1], (CB, 128))
        mb[i * CB : (i + 1) * CB, :] = jnp.broadcast_to(reads_wide[i : i + 1], (CB, HIST)).astype(BF)

    table_wait(S_REPLY, replies, False)
    got = replies[...].reshape(T * 2 * CAP, 128)
    history = jnp.concatenate([dot(pick_left, got), dot(pick_right, got)], axis=1)
    hist_scr[...] = history
    centred = history - jnp.mean(history, axis=1, keepdims=True)
    spread_v = jnp.mean(centred * centred, axis=1, keepdims=True)
    normed = (centred * lax.rsqrt(spread_v + 1e-5) * lngain_ref[...]).astype(BF)
    nown[0] = normed[:64]
    nown[1] = normed[64:]

    def normed_copy(dest, source):
        return pltpu.make_async_remote_copy(
            src_ref=nown.at[dest % 2],
            dst_ref=nall.at[source],
            send_sem=nsend.at[dest],
            recv_sem=nrecv.at[source],
            device_id=(t, dest),
            device_id_type=MESH,
        )

    def others(n):
        return lax.rem(k + n, K)

    for n in range(1, K):
        normed_copy(others(n), k).start()
    nall[k] = nown[core]
    pair_copy(0, wperm, 1 - core).wait_recv()
    pair_copy(1, gains, 1 - core).wait_recv()

    first = iota((128, 128), 1) < 64
    same_half = jnp.where((iota((128, 128), 0) < 64) == first, 1.0 / 64, 0.0).astype(BF)

    def project(chip):
        rows_n = nall[pl.ds(2 * chip, 2)].reshape(128, 256)
        place = pl.ds(pl.multiple_of(chip * 128, 128), 128)
        for p in range(2):
            out = silu_of_double(dot(rows_n, wperm[p])).astype(BF)
            values = out[:, 128:256]
            pv[p, place, :] = (values.astype(F32) - dot(values, same_half)).astype(BF)
            for n, ref in ((0, pg), (2, pq), (3, pk)):
                ref[p, place, :] = out[:, 128 * n : 128 * n + 128]

    normed_copy(sib, sib).wait_recv()
    project(x)
    for d in order:
        chip = lax.rem(x + d, X)
        for c in range(2):
            normed_copy(2 * chip + c, 2 * chip + c).wait_recv()
        project(chip)
    relay_finish(A_OUT, wo_all)
    relay_finish(A_K, wk_all)
    relay_finish(A_V, wv_all)
    relay_pass(A_CQ, wcq_all)
    relay_pass(A_CO, wco_all)
    relay_pass(A_MLP, wm_all)
    for n in range(X - 1):
        gather_pass(A_SCORE, ws_all, n)

    causal = (iota((256, 128), 0) & 127) >= iota((256, 128), 1)
    zero = jnp.zeros((128, 128), BF)

    def gated_copy(dest, source):
        return pltpu.make_async_remote_copy(
            src_ref=gs.at[dest],
            dst_ref=gall.at[source % 2, source // 2],
            send_sem=gsend.at[dest],
            recv_sem=grecv.at[source],
            device_id=(t, dest),
            device_id_type=MESH,
        )

    for group in ((0, 1), (2, 3)):
        for block in group:
            start = block * 128
            for p in range(2):
                queries = pq[p, start : start + 128, :] * 0.0625
                both = jnp.concatenate([jnp.where(first, queries, zero), jnp.where(first, zero, queries)], axis=0)
                half = dot_nt(both, pk[p, start : start + 128, :])
                weights = jnp.where(causal, silu_of_double(half), 0.0).astype(BF)
                total = dot(weights, pv[p, start : start + 128, :])
                if block:
                    weights = silu_of_double(dot_nt(both, pk[p, :start, :])).astype(BF)
                    total += dot(weights, pv[p, :start, :])
                off = jnp.where(first, total[:128], total[128:])
                spread_a = dot((off * off).astype(BF), same_half)
                gate = pg[p, start : start + 128, :].astype(F32)
                gated = (off * lax.rsqrt(spread_a + 1e-5) * gains[p] * gate).astype(BF)
                gs[2 * block, :, 128 * p : 128 * p + 128] = gated[:64]
                gs[2 * block + 1, :, 128 * p : 128 * p + 128] = gated[64:]
        for dest in [2 * block + half for block in group for half in range(2)]:

            @pl.when(k != dest)
            def _():
                gated_copy(dest, k).start()

    gall[core, x] = gs[k]

    relay_finish(A_CQ, wcq_all)
    for n in range(1, K):
        cand_copy(others(n), others(n)).wait_recv()
    gather_rest(A_CQ, wcq_all)
    locals_[2].wait()
    first_r = iota((TR, 128), 1) < 64
    zero_r = jnp.zeros((TR, 128), BF)

    def make_queries(j, carry):
        for tile in range(NT):
            cands = call[tile * SLOTS : (tile + 1) * SLOTS].reshape(TR, 256)
            queries = dot_nt(cands, wcq_all[j]).astype(BF) * 0.0625
            one = um[tile * TR : (tile + 1) * TR, :] > 0.5
            parts = (jnp.where(one, zero_r, queries), jnp.where(one, queries, zero_r))
            q2[j, tile, :TR, :] = jnp.concatenate([jnp.where(first_r, q, zero_r) for q in parts], axis=1)
            q2[j, tile, TR:, :] = jnp.concatenate([jnp.where(first_r, zero_r, q) for q in parts], axis=1)
        return carry

    lax.fori_loop(0, K // 2, make_queries, 0)

    gather_rest(A_OUT, wo_all)
    locals_[1].wait()
    for n in range(1, K):
        gated_copy(others(n), others(n)).wait_recv()
    total = hist_scr[...]
    for m in range(X):
        pieces = jnp.concatenate([gall[0, m], gall[1, m]], axis=0)
        total += dot(pieces, wo_all[2 * m : 2 * m + 2].reshape(256, 256))
    states = total.astype(BF)
    sall[k] = states
    gather_start(A_STATE, sall.at[k], sall)
    states_ref[...] = states.reshape(2, 64, 256)
    relay_finish(A_CO, wco_all)
    relay_finish(A_MLP, wm_all)

    lax.fori_loop(K // 2, K, make_queries, 0)

    gather_rest(A_K, wk_all)
    gather_rest(A_V, wv_all)

    def make_kv(part, own):
        place = slice(part * (HIST // 2), (part + 1) * (HIST // 2))
        values_w = jnp.concatenate([wv_all[j] for j in range(K)], axis=1)
        for u in range(2):
            rows_s = jnp.concatenate([sall[2 * m + own, 64 * u : 64 * u + 64, :] for m in range(X)], axis=0)
            keys = dot_nt(wk_all[...].reshape(K * 128, 256), rows_s).astype(BF)
            values = dot(rows_s, values_w).astype(BF)
            for j in range(K):
                k2[j, 128 * u : 128 * u + 128, place] = keys[128 * j : 128 * j + 128]
                v2[j, place, 128 * u : 128 * u + 128] = values[:, 128 * j : 128 * j + 128]

    for n in range(X - 1):
        gather_pass(A_STATE, sall, n)
    make_kv(0, core)
    gather_rest(A_STATE, sall)
    make_kv(1, 1 - core)

    def cross_pair(j, tile):
        tile_rows = pl.ds(pl.multiple_of(tile * TR, TR), TR)
        reads_t = mb[tile_rows, :]
        weights = silu_of_double(dot(q2[j, tile], k2[j])).astype(BF)
        weights = jnp.concatenate([weights[:TR] * reads_t, weights[TR:] * reads_t], axis=0)
        out = dot(weights, v2[j])
        one = um[tile_rows, :] > 0.5
        top = jnp.where(one, out[:TR, 128:], out[:TR, :128])
        bottom = jnp.where(one, out[TR:, 128:], out[TR:, :128])
        return jnp.where(first_r, top, bottom)

    gather_rest(A_CO, wco_all)
    gather_rest(A_MLP, wm_all)
    gather_rest(A_SCORE, ws_all)
    locals_[3].wait()
    locals_[4].wait()
    at_lane = iota((TR, 128), 0) % CB == iota((TR, 128), 1)

    def finish_tile(tile, carry):
        mixed = call[pl.ds(tile * SLOTS, SLOTS)].reshape(TR, 256).astype(F32)
        for m in range(X):
            pair = [
                (cross_pair(j, tile) * (1.0 / math.sqrt(HIST))).astype(BF)
                for j in (2 * m, 2 * m + 1)
            ]
            mixed += dot(jnp.concatenate(pair, axis=1), wco_all[2 * m : 2 * m + 2].reshape(256, 256))
        mixed = mixed.astype(BF)
        total_s = jnp.zeros((TR, 128), F32)
        for m in range(X):
            half = dot(mixed, jnp.concatenate([wm_all[2 * m], wm_all[2 * m + 1]], axis=1)) * 0.5
            hidden = silu_of_double(half).astype(BF).astype(F32)
            total_s += hidden[:, :128] * ws_all[2 * m][0:1, :] + hidden[:, 128:] * ws_all[2 * m + 1][0:1, :]
        score = jnp.sum(total_s, axis=1, keepdims=True)
        by_slot = jnp.sum(jnp.where(at_lane, score, 0.0).reshape(SLOTS, CB, 128), axis=1)
        sr[pl.ds(tile * SLOTS, SLOTS)] = by_slot.reshape(SLOTS, 1, 128)
        for i in range(SLOTS):
            for j in range(K):
                score_send(tile * SLOTS + i, j, lambda copy: copy.start())
        return carry

    def score_copy(slot, j, source):
        return pltpu.make_async_remote_copy(
            src_ref=sr.at[slot],
            dst_ref=rr.at[source],
            send_sem=tsend.at[S_SCORE, slot * K + j],
            recv_sem=trecv.at[S_SCORE, source],
            device_id=(SL * k + slot, j),
            device_id_type=MESH,
        )

    def score_send(slot, j, action):
        @pl.when((SL * k + slot != t) | (j != k))
        def _():
            action(score_copy(slot, j, t))

    lax.fori_loop(0, NT, finish_tile, 0)

    @pl.when(k == home)
    def _():
        rr[t] = sr[t - SL * k]

    table_wait(S_MSG, m1, True)
    table_wait(S_REPLY, replies, True)
    table_wait(S_CAND, cin, True)
    for n in range(1, K):
        cand_copy(others(n), k).wait_send()
    for a, buf in ((A_OUT, wo_all), (A_K, wk_all), (A_V, wv_all), (A_CQ, wcq_all), (A_CO, wco_all), (A_MLP, wm_all)):
        relay_drain(a, buf)
    gather_drain(A_SCORE, ws_all)
    gather_drain(A_STATE, sall)
    pair_copy(0, wperm, core).wait_send()
    pair_copy(1, gains, core).wait_send()
    for n in range(1, K):
        normed_copy(others(n), k).wait_send()
        gated_copy(others(n), k).wait_send()

    def score_wait(g, carry):
        @pl.when((g != t) | (k != home))
        def _():
            score_copy(0, 0, g).wait_recv()

        return carry

    lax.fori_loop(0, T, score_wait, 0)
    back = rr[...].reshape(T, 128)
    groups = iota((T, 128), 0)
    for b in range(4):
        scores_ref[b : b + 1, :] = jnp.sum(jnp.where(groups == group_s[b], back, 0.0), axis=0, keepdims=True)
    for slot in range(SL):
        for j in range(K):
            score_send(slot, j, lambda copy: copy.wait_send())


def body(
    T,
    K,
    table_rows,
    hist_owner,
    hist_row,
    ln_gain,
    w_proj,
    norm_gain,
    w_out,
    w_ckv,
    candidates,
    cand_group,
    cand_member,
    block_mask,
    w_cq,
    w_co,
    w_mlp,
    w_score,
):
    slab = table_rows.shape[0]
    cap = max(1, 2 * hist_owner.size // T)
    rows, hist = 16 * T, 64 * K
    tile = min(rows, 256)
    vmem, hbm = pl.BlockSpec(memory_space=pltpu.VMEM), pl.BlockSpec(memory_space=pltpu.HBM)
    scratch = [
        pltpu.SMEM((4,), I32),
        pltpu.SMEM((4,), I32),
        pltpu.SMEM((4, 4), I32),
        pltpu.VMEM((2, 64), I32),
        pltpu.VMEM((2, 64), I32),
        pltpu.VMEM((1, 256), F32),
        pltpu.VMEM((256, 2, 256), BF),
        pltpu.VMEM((2, 64), F32),
        pltpu.VMEM((256, 2, 128), BF),
        pltpu.VMEM((64 * K, 256), BF),
        pltpu.VMEM((1, 128), BF),
        pltpu.VMEM((slab, 256), BF),
        pltpu.VMEM((2, 128), I32),
        pltpu.VMEM((T, 2, 128), I32),
        pltpu.VMEM((T, 2 * cap, 128), BF),
        pltpu.VMEM((T, 2 * cap, 128), BF),
        pltpu.VMEM((T, 16, 256), BF),
        pltpu.VMEM((T, 16, 256), BF),
        pltpu.VMEM((T // K, 16 * K, 256), BF),
        pltpu.VMEM((2, 256, 512), BF),
        pltpu.VMEM((2, 1, 128), F32),
        pltpu.VMEM((K, 128, 256), BF),
        pltpu.VMEM((K, 128, 256), BF),
        pltpu.VMEM((K, 256, 128), BF),
        pltpu.VMEM((K, 128, 256), BF),
        pltpu.VMEM((K, 128, 256), BF),
        pltpu.VMEM((K, 256, 128), BF),
        pltpu.VMEM((K, 8, 128), F32),
        pltpu.VMEM((128, 256), F32),
        pltpu.VMEM((2, 64, 256), BF),
        pltpu.VMEM((K, 64, 256), BF),
        pltpu.VMEM((2, hist, 128), BF),
        pltpu.VMEM((2, hist, 128), BF),
        pltpu.VMEM((2, hist, 128), BF),
        pltpu.VMEM((2, hist, 128), BF),
        pltpu.VMEM((K, 64, 256), BF),
        pltpu.VMEM((2, K // 2, 64, 256), BF),
        pltpu.VMEM((K, 128, 256), BF),
        pltpu.VMEM((K, rows // tile, 2 * tile, 256), BF),
        pltpu.VMEM((K, 256, hist), BF),
        pltpu.VMEM((K, hist, 256), BF),
        pltpu.VMEM((rows, hist), BF),
        pltpu.VMEM((rows, 128), F32),
        pltpu.VMEM((T // K, 1, 128), F32),
        pltpu.VMEM((T, 1, 128), F32),
        pltpu.SemaphoreType.DMA((16,)),
        pltpu.SemaphoreType.DMA((4, T)),
        pltpu.SemaphoreType.DMA((4, T)),
        pltpu.SemaphoreType.DMA((8, K)),
        pltpu.SemaphoreType.DMA((8, K)),
        pltpu.SemaphoreType.DMA((8, 2)),
        pltpu.SemaphoreType.DMA((2, K)),
        pltpu.SemaphoreType.DMA((2,)),
        pltpu.SemaphoreType.DMA((2,)),
        pltpu.SemaphoreType.DMA((K,)),
        pltpu.SemaphoreType.DMA((K,)),
        pltpu.SemaphoreType.DMA((K,)),
        pltpu.SemaphoreType.DMA((K,)),
    ]
    states, scores = pl.pallas_call(
        functools.partial(kernel, T, K, slab, cap),
        out_shape=(
            jax.ShapeDtypeStruct((2, 64, 256), BF),
            jax.ShapeDtypeStruct((4, 128), F32),
        ),
        in_specs=[hbm] * 16,
        out_specs=(vmem, vmem),
        scratch_shapes=scratch,
        compiler_params=pltpu.CompilerParams(
            collective_id=0, has_side_effects=True, vmem_limit_bytes=60 * 1024 * 1024
        ),
    )(
        cand_group,
        cand_member,
        block_mask,
        hist_owner,
        hist_row,
        ln_gain.reshape(1, 256),
        w_proj,
        norm_gain,
        w_ckv,
        candidates,
        w_score.reshape(1, 128),
        table_rows,
        w_out.reshape(128, 256),
        jnp.transpose(w_cq, (1, 2, 0)).reshape(128, 256),
        w_co.reshape(128, 256),
        w_mlp,
    )
    return states, scores[:, : 16 * K].reshape(4 * 16 * K)


def solution(mesh):
    T, K = mesh.shape["table"], mesh.shape["tensor"]
    return jax.shard_map(
        functools.partial(body, T, K),
        mesh=mesh,
        in_specs=(
            P("table", None),
            P("table", "tensor"),
            P("table", "tensor"),
            P(),
            P(None, "tensor", None),
            P("tensor", None),
            P("tensor", None, None),
            P(None, "tensor", None),
            P("table", None),
            P("table"),
            P("table"),
            P("table", None),
            P(None, "tensor", None),
            P("tensor", None, None),
            P(None, "tensor"),
            P("tensor"),
        ),
        out_specs=(P("table", "tensor", None), P("table")),
        check_vma=False,
    )
```
